256 devices in a mesh: seq: 64 (over z, y, core), head: 4 (over x).
Axes of the slice: x: 4, y: 4, z: 8, core: 2. Of those that a mesh axis runs over, the one named last changes fastest.
Arguments:
- video_tokens: bfloat16 [32768, 3072], P('seq'), may hold values from -56 to 56
- text_tokens: bfloat16 [256, 3072], P('seq'), may hold values from -6 to 6
- project_in: bfloat16 [3072, 12, 384], P(None, 'head'), may hold values from -0.1875 to 0.1875
- project_out: bfloat16 [12, 128, 3072], P('head'), may hold values from -0.15625 to 0.15625
- head_class: int32 [12], replicated, may hold values from 0 to 1, as said below
- text_length: int32 [1], replicated, may hold values from 32 to 256
Outputs:
- block_output: bfloat16 [32768, 3072], P(('seq', 'head'))
The draws below stay inside these ranges and needn't reach their ends.
Inputs may be any that keep to these rules, and one draw needn't show every extreme that they name: `head_class`: 1 marks a spatial head and 0 a temporal one; from 3 to 9 heads are spatial, which ones varies. The first text_length text slots hold real text, the others padding.
All inputs are finite; a program needn't handle non-finite values.
Results may differ from the reference program's by a relative error of at most 0.006.
The reference program's roundings to bfloat16 on the way count: a program that leaves them out, or rounds other values in their place, can miss the bound.
Values may be sent and summed in bfloat16 or wider, within the bound.
No kernel may reach another device: no remote copies, remote signals or barrier semaphores. Data moves between devices by JAX's collectives and lax.ppermute only.
A program may use at most 128 MiB of HBM per device.

```python
import jax
import jax.numpy as jnp
from jax import lax

D = 3072
HEADS = 12
HD = 128
TEXT = 256
FRAME_LEN = 1024
FRAMES = 32
TOKENS = 32768


def draw_video_tokens(key, part):
    key = jax.random.fold_in(key, 5)
    entries = jax.random.normal(key, (TOKENS, D), jnp.float32)
    return jnp.clip(entries, -4.0, 4.0).astype(jnp.bfloat16)


def draw_head_class(key, part):
    key = jax.random.fold_in(key, 11)
    key_count, key_order = jax.random.split(key)
    spatial_count = jax.random.randint(key_count, (), HEADS // 4, 3 * HEADS // 4 + 1)
    ordering = jax.random.permutation(key_order, HEADS)
    return (ordering < spatial_count).astype(jnp.int32)


def block_scale(key, dims, cuts, smallest, largest):
    factor_of = 1.0
    for dim, shards_of in cuts:
        heights = jax.random.uniform(jax.random.fold_in(jax.random.fold_in(key, 6), dim), (shards_of,), jnp.float32, smallest / len(cuts), largest / len(cuts))
        factor_of = factor_of * jnp.repeat(jnp.exp(heights), dims[dim] // shards_of).reshape((-1,) + (1,) * (len(dims) - 1 - dim))
    return factor_of


def normal_values(stream_key, extent, scale, bound, pieces=(), kind=jnp.bfloat16):
    gain = block_scale(stream_key, extent, pieces, -0.22, 0.18) if pieces else 1.0
    result = jax.random.normal(stream_key, extent, jnp.float32) * scale * gain
    return jnp.minimum(jnp.maximum(result, -bound), bound).astype(kind)


def setup_inputs(seed: int = 0) -> dict:
    streams_of = jax.random.split(jax.random.key(seed), 7)
    return {
        "video_tokens": draw_video_tokens(jax.random.fold_in(streams_of[6], 71), 0),
        "text_tokens": normal_values(streams_of[1], (TEXT, D), 1.0, 6.0, ((0, 64),)),
        "project_in": normal_values(streams_of[2], (D, HEADS, 3 * HD), (D // 3) ** -0.5, 0.1875, ((1, 4),)),
        "project_out": normal_values(streams_of[3], (HEADS, HD, D), (HEADS * HD) ** -0.5, 0.15625, ((0, 4),)),
        "head_class": draw_head_class(jax.random.fold_in(streams_of[6], 71), 0),
        "text_length": jax.random.randint(streams_of[5], (1,), TEXT // 8, TEXT + 1).astype(jnp.int32),
    }


masked_score = -1.0e30


def soft_attend(query_rows, key_rows, value_rows, key_valid, score_scale):
    scores = jnp.einsum("qd,kd->qk", query_rows, key_rows, precision=lax.Precision.HIGHEST) * score_scale
    scores = jnp.where(key_valid[None, :], scores, masked_score)
    highest = jnp.max(scores, axis=1, keepdims=True)
    weights = jnp.exp(scores - highest)
    totals = jnp.sum(weights, axis=1, keepdims=True)
    rounded = lax.optimization_barrier(weights.astype(jnp.bfloat16)).astype(jnp.float32)
    summed = jnp.einsum("qk,kd->qd", rounded, value_rows, precision=lax.Precision.HIGHEST)
    return (summed / totals).astype(jnp.bfloat16)


def reference(video_tokens, text_tokens, project_in, project_out, head_class, text_length):
    score_scale = HD ** -0.5
    flat_in = project_in.reshape(D, HEADS * 3 * HD)
    packed = jnp.dot(video_tokens, flat_in, preferred_element_type=jnp.float32).astype(jnp.bfloat16)
    packed = packed.reshape(TOKENS, HEADS, 3 * HD)
    text_packed = jnp.dot(text_tokens, flat_in, preferred_element_type=jnp.float32).astype(jnp.bfloat16)
    text_packed = text_packed.reshape(TEXT, HEADS, 3 * HD)
    text_valid = jnp.arange(TEXT, dtype=jnp.int32) < text_length[0]

    def spatial(query_rows, key_rows, value_rows, text_keys, text_values):
        first_keys = key_rows[:FRAME_LEN]
        first_values = value_rows[:FRAME_LEN]

        def one_frame(frame_index):
            start = (frame_index * FRAME_LEN).astype(jnp.int32)
            own_queries = lax.dynamic_slice_in_dim(query_rows, start, FRAME_LEN, 0)
            own_keys = lax.dynamic_slice_in_dim(key_rows, start, FRAME_LEN, 0)
            own_values = lax.dynamic_slice_in_dim(value_rows, start, FRAME_LEN, 0)
            all_keys = jnp.concatenate([own_keys, first_keys, text_keys], axis=0)
            all_values = jnp.concatenate([own_values, first_values, text_values], axis=0)
            key_valid = jnp.concatenate([jnp.ones((FRAME_LEN,), bool), jnp.broadcast_to(frame_index != 0, (FRAME_LEN,)), text_valid])
            return soft_attend(own_queries, all_keys, all_values, key_valid, score_scale)

        return lax.map(one_frame, jnp.arange(FRAMES, dtype=jnp.int32)).reshape(TOKENS, HD)

    def temporal(query_rows, key_rows, value_rows, text_keys, text_values):
        query_grid = query_rows.reshape(FRAMES, FRAME_LEN, HD)
        key_grid = key_rows.reshape(FRAMES, FRAME_LEN, HD)
        value_grid = value_rows.reshape(FRAMES, FRAME_LEN, HD)
        frame_scores = jnp.einsum("fpd,epd->fpe", query_grid, key_grid, precision=lax.Precision.HIGHEST) * score_scale
        text_scores = jnp.einsum("fpd,sd->fps", query_grid, text_keys, precision=lax.Precision.HIGHEST) * score_scale
        text_scores = jnp.where(text_valid[None, None, :], text_scores, masked_score)
        highest = jnp.maximum(jnp.max(frame_scores, axis=2), jnp.max(text_scores, axis=2))[:, :, None]
        frame_weights = jnp.exp(frame_scores - highest)
        text_weights = jnp.exp(text_scores - highest)
        totals = jnp.sum(frame_weights, axis=2) + jnp.sum(text_weights, axis=2)
        frame_rounded = lax.optimization_barrier(frame_weights.astype(jnp.bfloat16)).astype(jnp.float32)
        text_rounded = lax.optimization_barrier(text_weights.astype(jnp.bfloat16)).astype(jnp.float32)
        summed = jnp.einsum("fpe,epd->fpd", frame_rounded, value_grid, precision=lax.Precision.HIGHEST)
        summed = summed + jnp.einsum("fps,sd->fpd", text_rounded, text_values, precision=lax.Precision.HIGHEST)
        return (summed / totals[:, :, None]).astype(jnp.bfloat16).reshape(TOKENS, HD)

    def one_head(head_index):
        column = lax.dynamic_index_in_dim(packed, head_index, 1, keepdims=False).astype(jnp.float32)
        text_column = lax.dynamic_index_in_dim(text_packed, head_index, 1, keepdims=False).astype(jnp.float32)
        query_rows = column[:, :HD]
        key_rows = column[:, HD:2 * HD]
        value_rows = column[:, 2 * HD:]
        text_keys = text_column[:, HD:2 * HD]
        text_values = text_column[:, 2 * HD:]
        return lax.cond(head_class[head_index] == 1, spatial, temporal, query_rows, key_rows, value_rows, text_keys, text_values)

    per_head = lax.map(one_head, jnp.arange(HEADS, dtype=jnp.int32))
    attention = jnp.transpose(per_head, (1, 0, 2)).reshape(TOKENS, HEADS * HD)
    block_output = jnp.dot(attention, project_out.reshape(HEADS * HD, D), preferred_element_type=jnp.float32)
    return block_output.astype(jnp.bfloat16)
```

```python
import functools
import math

import jax
import jax.numpy as jnp
from jax import lax
from jax.experimental import pallas as pl
from jax.experimental.pallas import tpu as pltpu
from jax.sharding import Mesh, PartitionSpec as P

Z, Y, CORES, PLANES = 8, 4, 2, 4
CHIPS = Z * Y
HEADS_HERE = 3
HEAD = 128
TRIPLE = 3 * HEAD
ROWS = 512
PIECE = ROWS // CHIPS
TEXT_HERE = 4
TEXT_CORE = CHIPS * TEXT_HERE
TOKEN_PART = HEADS_HERE * PIECE
CHUNK = TOKEN_PART + 2 * TEXT_HERE
WIDTH = 3072
MASKED = -1e30
FACTOR = HEAD**-0.5 * math.log2(math.e)
VMEM_LIMIT = 48 * 1024 * 1024

f32 = jnp.float32
bf16 = jnp.bfloat16


def params(**kw):
    return pltpu.CompilerParams(vmem_limit_bytes=VMEM_LIMIT, **kw)


def nt(a, b):
    return lax.dot_general(a, b, (((1,), (1,)), ((), ())), preferred_element_type=f32)


def project_kernel(x_ref, text_ref, w_ref, out_ref, text_rows):
    head = pl.program_id(0)
    w = w_ref[0]
    rows = jnp.dot(x_ref[...], w, preferred_element_type=f32).astype(bf16)
    rows = rows.reshape(CHIPS, PIECE, TRIPLE)
    text = jnp.dot(text_ref[...], w, preferred_element_type=f32)
    for h in range(HEADS_HERE):

        @pl.when(head == h)
        def _():
            out_ref[:, h * PIECE : (h + 1) * PIECE, :] = rows
            lanes = slice(h * HEAD, (h + 1) * HEAD)
            text_rows[0:TEXT_HERE, lanes] = text[:, HEAD : 2 * HEAD]
            text_rows[TEXT_HERE : 2 * TEXT_HERE, lanes] = text[:, 2 * HEAD :]

    @pl.when(head == HEADS_HERE - 1)
    def _():
        out_ref[:, TOKEN_PART:, :] = jnp.broadcast_to(
            text_rows[...].astype(bf16)[None], (CHIPS, 2 * TEXT_HERE, TRIPLE)
        )


def project(video_tokens, text_tokens, weights):
    return pl.pallas_call(
        project_kernel,
        grid=(HEADS_HERE,),
        in_specs=[
            pl.BlockSpec((ROWS, WIDTH), lambda h: (0, 0)),
            pl.BlockSpec((TEXT_HERE, WIDTH), lambda h: (0, 0)),
            pl.BlockSpec((1, WIDTH, TRIPLE), lambda h: (h, 0, 0)),
        ],
        out_specs=pl.BlockSpec((CHIPS, CHUNK, TRIPLE), lambda h: (0, 0, 0)),
        out_shape=jax.ShapeDtypeStruct((CHIPS, CHUNK, TRIPLE), bf16),
        scratch_shapes=[pltpu.VMEM((2 * TEXT_HERE, TRIPLE), f32)],
        compiler_params=params(),
        cost_estimate=pl.CostEstimate(
            flops=2 * ROWS * WIDTH * 3 * TRIPLE, bytes_accessed=12_000_000, transcendentals=0
        ),
        name="project",
    )(video_tokens, text_tokens, weights)


def text_slots(rows, core):
    place = lax.broadcasted_iota(jnp.int32, (rows, TEXT_CORE), 1)
    return (
        lax.shift_right_logical(place, 2) * (CORES * TEXT_HERE) + core * TEXT_HERE + (place & 3)
    )


def text_scores(query, keys, core, length):
    scores = nt(query, keys)
    return jnp.where(text_slots(query.shape[0], core) < length, scores, MASKED)


def finish(parts, values, shifts=None):
    highest = functools.reduce(
        jnp.maximum, [jnp.max(s, axis=1, keepdims=True) for s in parts]
    )
    top = highest * FACTOR
    total = 0.0
    summed = 0.0
    for index, (s, v) in enumerate(zip(parts, values)):
        low = top if shifts is None or shifts[index] is None else top + shifts[index]
        w = jnp.exp2(s * FACTOR - low)
        total = total + jnp.sum(w, axis=1, keepdims=True)
        summed = summed + jnp.dot(w.astype(bf16), v, preferred_element_type=f32)
    return (summed / total).astype(bf16)


def temporal_kernel(info, rows_ref, text_a, text_b, out_ref):
    head = pl.program_id(0)
    core, length = info[3], info[4]

    @pl.when(info[head] == 0)
    def _():
        block = rows_ref[...].reshape(ROWS, TRIPLE)
        keys = block[:, HEAD : 2 * HEAD]
        values = block[:, 2 * HEAD :]
        step = 128
        for start in range(0, ROWS, step):
            query = block[start : start + step, :HEAD]
            scores = nt(query, keys)
            own = lax.broadcasted_iota(jnp.int32, scores.shape, 0) & (PIECE - 1)
            other = lax.broadcasted_iota(jnp.int32, scores.shape, 1) & (PIECE - 1)
            scores = jnp.where(own == other, scores, MASKED)
            result = finish(
                [
                    scores,
                    text_scores(query, text_a[0], core, length),
                    text_scores(query, text_b[0], 1 - core, length),
                ],
                [values, text_a[1], text_b[1]],
            )
            count = step // PIECE
            place = start // PIECE
            out_ref[place : place + count] = result.reshape(count, PIECE, HEAD)

    @pl.when(info[head] != 0)
    def _():
        out_ref[...] = jnp.zeros_like(out_ref)


def temporal(info, rows, text_a, text_b):
    text_spec = pl.BlockSpec((2, TEXT_CORE, HEAD), lambda h, _: (0, 0, h))
    return pl.pallas_call(
        temporal_kernel,
        grid_spec=pltpu.PrefetchScalarGridSpec(
            num_scalar_prefetch=1,
            grid=(HEADS_HERE,),
            in_specs=[
                pl.BlockSpec((CHIPS, PIECE, TRIPLE), lambda h, _: (0, h, 0)),
                text_spec,
                text_spec,
            ],
            out_specs=pl.BlockSpec((CHIPS, PIECE, HEAD), lambda h, _: (0, h, 0)),
        ),
        out_shape=jax.ShapeDtypeStruct((CHIPS, TOKEN_PART, HEAD), bf16),
        compiler_params=params(),
        cost_estimate=pl.CostEstimate(
            flops=400_000_000, bytes_accessed=3_000_000, transcendentals=1_200_000
        ),
        name="temporal",
    )(info, rows, text_a, text_b)


def spatial_kernel(info, own, partner, first_a, first_b, text_a, text_b, back, out_ref):
    head = pl.program_id(0)
    core, length, frame = info[3], info[4], info[5]

    @pl.when(info[head] != 0)
    def _():
        shift = jnp.where(frame == 0, -MASKED, 0.0).astype(f32)
        step = 128

        def body(index, _):
            count = step // PIECE
            query = own[pl.ds(index * count, count), :, :HEAD].reshape(step, HEAD)
            pairs = []
            for ref, at in ((own, 1), (partner, 1), (first_a, 0), (first_b, 0)):
                keys = ref[:, :, at * HEAD : (at + 1) * HEAD].reshape(ROWS, HEAD)
                values = ref[:, :, (at + 1) * HEAD : (at + 2) * HEAD].reshape(ROWS, HEAD)
                pairs.append((nt(query, keys), values))
            pairs.append((text_scores(query, text_a[0], core, length), text_a[1]))
            pairs.append((text_scores(query, text_b[0], 1 - core, length), text_b[1]))
            result = finish(
                [p[0] for p in pairs],
                [p[1] for p in pairs],
                [None, None, shift, shift, None, None],
            )
            out_ref[pl.ds(pl.multiple_of(index * step, step), step), :] = result
            return 0

        lax.fori_loop(0, ROWS // step, body, 0)

    @pl.when(info[head] == 0)
    def _():
        out_ref[...] = back[...].reshape(ROWS, HEAD)


def spatial(info, own, partner, first_a, first_b, text_a, text_b, back):
    text_spec = pl.BlockSpec((2, TEXT_CORE, HEAD), lambda h, _: (0, 0, h))
    packed_spec = pl.BlockSpec((CHIPS, PIECE, TRIPLE), lambda h, _: (0, h, 0))
    first_spec = pl.BlockSpec((CHIPS, PIECE, 2 * HEAD), lambda h, _: (0, h, 0))
    return pl.pallas_call(
        spatial_kernel,
        grid_spec=pltpu.PrefetchScalarGridSpec(
            num_scalar_prefetch=1,
            grid=(HEADS_HERE,),
            in_specs=[
                packed_spec,
                packed_spec,
                first_spec,
                first_spec,
                text_spec,
                text_spec,
                pl.BlockSpec((CHIPS, PIECE, HEAD), lambda h, _: (0, h, 0)),
            ],
            out_specs=pl.BlockSpec((ROWS, HEAD), lambda h, _: (0, h)),
        ),
        out_shape=jax.ShapeDtypeStruct((ROWS, TRIPLE), bf16),
        compiler_params=params(),
        cost_estimate=pl.CostEstimate(
            flops=1_800_000_000, bytes_accessed=6_000_000, transcendentals=3_600_000
        ),
        name="spatial",
    )(info, own, partner, first_a, first_b, text_a, text_b, back)


def out_kernel(place, rows_ref, own, a1, a2, a3, b1, b2, b3, out_ref):
    plane = place[0]
    half = pl.program_id(0)

    def partial(index, w):
        rows = rows_ref[(plane + PLANES - index) % PLANES]
        return jnp.dot(rows, w[...], preferred_element_type=f32)

    base = partial(0, own)

    @pl.when(half == 0)
    def _():
        total = base + partial(1, a1) + partial(2, a2) + partial(3, a3)
        out_ref[...] = total.astype(bf16)

    @pl.when(half == 1)
    def _():
        total = base + partial(1, b1) + partial(2, b2) + partial(3, b3)
        out_ref[...] = total.astype(bf16)


def out_project(place, rows, own, mine, theirs):
    wide = 512
    count = WIDTH // CORES // wide

    def column(half, n, place):
        return (0, jnp.where(half == 0, place[1], 1 - place[1]) * count + n)

    mine_spec = pl.BlockSpec(
        (TRIPLE, wide), lambda half, n, place: (0, jnp.where(half == 0, n, count - 1))
    )
    theirs_spec = pl.BlockSpec(
        (TRIPLE, wide), lambda half, n, place: (0, jnp.where(half == 0, 0, n))
    )
    out_rows = rows.shape[1]
    return pl.pallas_call(
        out_kernel,
        grid_spec=pltpu.PrefetchScalarGridSpec(
            num_scalar_prefetch=1,
            grid=(CORES, count),
            in_specs=[
                pl.BlockSpec(rows.shape, lambda half, n, place: (0, 0, 0)),
                pl.BlockSpec((TRIPLE, wide), column),
            ]
            + [mine_spec] * 3
            + [theirs_spec] * 3,
            out_specs=pl.BlockSpec((out_rows, wide), column),
        ),
        out_shape=jax.ShapeDtypeStruct((out_rows, WIDTH), bf16),
        compiler_params=params(),
        cost_estimate=pl.CostEstimate(
            flops=2 * out_rows * 1536 * WIDTH, bytes_accessed=10_500_000, transcendentals=0
        ),
        name="out_project",
    )(place, rows, own, *mine, *theirs)


def swap_cores(value):
    return lax.ppermute(value, "core", [(0, 1), (1, 0)])


def local(video_tokens, text_tokens, project_in, project_out, head_class, text_length):
    z, y = lax.axis_index("z"), lax.axis_index("y")
    core, plane = lax.axis_index("core"), lax.axis_index("head")
    here = lax.dynamic_slice_in_dim(head_class, plane * HEADS_HERE, HEADS_HERE)
    info = jnp.concatenate([here, jnp.stack([core, text_length[0], z * Y + y, 0, 0])])
    place = jnp.stack([plane, core])

    own_out = project_out.reshape(TRIPLE, WIDTH)
    half_out = lax.dynamic_slice_in_dim(own_out, core * (WIDTH // CORES), WIDTH // CORES, 1)
    mine = [
        lax.ppermute(half_out, "head", [(i, (i + k) % PLANES) for i in range(PLANES)])
        for k in (1, 2, 3)
    ]
    theirs = [swap_cores(m) for m in mine]

    weights = jnp.transpose(project_in, (1, 0, 2))
    packed = project(video_tokens, text_tokens, weights)
    moved = lax.all_to_all(packed, ("z", "y"), 0, 0, tiled=True)
    partner = swap_cores(packed)

    text_part = moved[:, TOKEN_PART:, :].reshape(CHIPS, 2, TEXT_HERE, TRIPLE)
    text_a = jnp.transpose(text_part, (1, 0, 2, 3)).reshape(2, TEXT_CORE, TRIPLE)
    text_b = swap_cores(text_a)

    first_piece = moved[0, :TOKEN_PART, HEAD:]
    copies = jnp.broadcast_to(first_piece[None], (Z,) + first_piece.shape)
    column = lax.all_to_all(copies, "z", 0, 0, tiled=True)
    copies = jnp.broadcast_to(column[None], (Y,) + column.shape)
    first_a = lax.all_to_all(copies, "y", 0, 0, tiled=True).reshape(
        CHIPS, TOKEN_PART, 2 * HEAD
    )
    first_b = swap_cores(first_a)

    over_time = temporal(info, moved, text_a, text_b)
    back = lax.all_to_all(over_time, ("z", "y"), 0, 0, tiled=True)
    attention = spatial(info, packed, partner, first_a, first_b, text_a, text_b, back)

    gathered = lax.all_to_all(
        attention.reshape(PLANES, ROWS // PLANES, TRIPLE), "head", 0, 0, tiled=True
    )
    return out_project(place, gathered, own_out, mine, theirs)


def solution(mesh):
    split = Mesh(mesh.devices.reshape(Z, Y, CORES, PLANES), ("z", "y", "core", "head"))
    seq = ("z", "y", "core")
    placed = (
        P(seq, None),
        P(seq, None),
        P(None, "head", None),
        P("head", None, None),
        P(),
        P(),
    )
    return jax.shard_map(
        local, mesh=split, in_specs=placed, out_specs=P(seq + ("head",), None), check_vma=False
    )
```

```python
import functools
import math

import jax
import jax.numpy as jnp
from jax import lax
from jax.experimental import pallas as pl
from jax.experimental.pallas import tpu as pltpu
from jax.sharding import Mesh, PartitionSpec as P

Z, Y, CORES, PLANES = 8, 4, 2, 4
CHIPS = Z * Y
HEADS_HERE = 3
HEAD = 128
TRIPLE = 3 * HEAD
ROWS = 512
BLOCK = ROWS // PLANES
PIECE = ROWS // CHIPS
TEXT_HERE = 4
TEXT_CORE = CHIPS * TEXT_HERE
TOKEN_PART = HEADS_HERE * PIECE
CHUNK = TOKEN_PART + 2 * TEXT_HERE
WIDTH = 3072
MASKED = -1e30
FACTOR = HEAD**-0.5 * math.log2(math.e)
MIB = 1024 * 1024

f32 = jnp.float32
bf16 = jnp.bfloat16


def params(mib):
    return pltpu.CompilerParams(vmem_limit_bytes=mib * MIB)


def nt(a, b):
    return lax.dot_general(a, b, (((1,), (1,)), ((), ())), preferred_element_type=f32)


CUTS = ((0, 768), (768, 2304))
TALL = ROWS + 16


def project_kernel(x_hbm, text_ref, w_hbm, out_ref, x, w, total, text_rows, x_sem, w_sem):
    def fetch(part):
        depth = pl.ds(*CUTS[part])
        yield pltpu.make_async_copy(x_hbm.at[:, depth], x.at[pl.ds(0, ROWS), depth], x_sem.at[part])
        for h in range(HEADS_HERE):
            lanes = pl.ds(h * TRIPLE, TRIPLE)
            yield pltpu.make_async_copy(
                w_hbm.at[h, depth], w.at[depth, lanes], w_sem.at[part, h]
            )

    for part in range(len(CUTS)):
        for copy in fetch(part):
            copy.start()
    padding = jnp.zeros((TALL - ROWS - TEXT_HERE, WIDTH), f32)
    x[ROWS:, :] = jnp.concatenate([text_ref[...].astype(f32), padding], axis=0).astype(bf16)

    def partial(part):
        for copy in fetch(part):
            copy.wait()
        first, depth = CUTS[part]
        return jnp.dot(
            x[:, first : first + depth], w[first : first + depth, :], preferred_element_type=f32
        )

    total[...] = partial(0)
    rows = total[...] + partial(1)
    for h in range(HEADS_HERE):
        lanes = slice(h * TRIPLE, (h + 1) * TRIPLE)
        piece = rows[:ROWS, lanes].astype(bf16)
        out_ref[:, h * PIECE : (h + 1) * PIECE, :] = piece.reshape(CHIPS, PIECE, TRIPLE)
        text = rows[ROWS : ROWS + 8, lanes]
        lanes = slice(h * HEAD, (h + 1) * HEAD)
        text_rows[0:TEXT_HERE, lanes] = text[0:TEXT_HERE, HEAD : 2 * HEAD]
        text_rows[TEXT_HERE : 2 * TEXT_HERE, lanes] = text[0:TEXT_HERE, 2 * HEAD :]
    out_ref[:, TOKEN_PART:, :] = jnp.broadcast_to(
        text_rows[...].astype(bf16)[None], (CHIPS, 2 * TEXT_HERE, TRIPLE)
    )


def project(video_tokens, text_tokens, weights):
    vmem = pl.BlockSpec(memory_space=pltpu.VMEM)
    hbm = pl.BlockSpec(memory_space=pltpu.HBM)
    return pl.pallas_call(
        project_kernel,
        in_specs=[hbm, vmem, hbm],
        out_specs=vmem,
        out_shape=jax.ShapeDtypeStruct((CHIPS, CHUNK, TRIPLE), bf16),
        scratch_shapes=[
            pltpu.VMEM((TALL, WIDTH), bf16),
            pltpu.VMEM((WIDTH, HEADS_HERE * TRIPLE), bf16),
            pltpu.VMEM((TALL, HEADS_HERE * TRIPLE), f32),
            pltpu.VMEM((2 * TEXT_HERE, TRIPLE), f32),
            pltpu.SemaphoreType.DMA((len(CUTS),)),
            pltpu.SemaphoreType.DMA((len(CUTS), HEADS_HERE)),
        ],
        compiler_params=params(62),
        cost_estimate=pl.CostEstimate(
            flops=2 * ROWS * WIDTH * 3 * TRIPLE, bytes_accessed=12_000_000, transcendentals=0
        ),
        name="project",
    )(video_tokens, text_tokens, weights)


def text_slots(rows, core):
    row = lax.broadcasted_iota(jnp.int32, (rows, TEXT_CORE), 1)
    chip = row & (CHIPS - 1)
    return chip * (CORES * TEXT_HERE) + core * TEXT_HERE + lax.shift_right_logical(row, 5)


def weigh(scores, top, values, total, summed):
    weights = jnp.exp2(scores * FACTOR - top)
    total = total + jnp.sum(weights, axis=1, keepdims=True)
    summed = summed + jnp.dot(weights.astype(bf16), values, preferred_element_type=f32)
    return total, summed


def mask_text(scores, core, length):
    slots = jnp.concatenate(
        [text_slots(scores.shape[0], core), text_slots(scores.shape[0], 1 - core)], axis=1
    )
    return jnp.where(slots < length, scores, MASKED)


def temporal_kernel(info, rows_ref, text_own, text_other, out_ref, text_ref, spread):
    core, length = info[3], info[4]

    for side, source in enumerate((text_own, text_other)):
        for h in range(HEADS_HERE):
            lanes = source[:, :, h * HEAD : (h + 1) * HEAD].astype(f32)
            spread[...] = lanes.reshape(CHIPS * 2 * TEXT_HERE, HEAD)
            for kind in range(2):
                for t in range(TEXT_HERE):
                    rows = pl.ds(kind * TEXT_HERE + t, CHIPS, stride=2 * TEXT_HERE)
                    first = side * TEXT_CORE + t * CHIPS
                    text_ref[h, kind, first : first + CHIPS, :] = spread[rows, :].astype(bf16)

    step = 128
    count = step // PIECE
    for h in range(HEADS_HERE):
        part = slice(h * PIECE, (h + 1) * PIECE)

        @pl.when(info[h] == 0)
        def _():
            keys = rows_ref[:, part, HEAD : 2 * HEAD].reshape(ROWS, HEAD)
            values = rows_ref[:, part, 2 * HEAD :].reshape(ROWS, HEAD)
            for index in range(ROWS // step):
                chips = slice(index * count, (index + 1) * count)
                query = rows_ref[chips, part, :HEAD].reshape(step, HEAD)
                scores = nt(query, keys)
                own = lax.broadcasted_iota(jnp.int32, scores.shape, 0) & (PIECE - 1)
                other = lax.broadcasted_iota(jnp.int32, scores.shape, 1) & (PIECE - 1)
                scores = jnp.where(own == other, scores, MASKED)
                text = mask_text(nt(query, text_ref[h, 0]), core, length)
                top = FACTOR * jnp.maximum(
                    jnp.max(scores, axis=1, keepdims=True), jnp.max(text, axis=1, keepdims=True)
                )
                total, summed = weigh(scores, top, values, 0.0, 0.0)
                total, summed = weigh(text, top, text_ref[h, 1], total, summed)
                result = (summed / total).astype(bf16)
                out_ref[chips, part, :] = result.reshape(count, PIECE, HEAD)

        @pl.when(info[h] != 0)
        def _():
            out_ref[:, part, :] = jnp.zeros((CHIPS, PIECE, HEAD), bf16)


def specs(count):
    return [pl.BlockSpec(memory_space=pltpu.SMEM)] + [
        pl.BlockSpec(memory_space=pltpu.VMEM)
    ] * count


def temporal(info, rows, text_own, text_other):
    return pl.pallas_call(
        temporal_kernel,
        in_specs=specs(3),
        out_specs=[pl.BlockSpec(memory_space=pltpu.VMEM)] * 2,
        out_shape=[
            jax.ShapeDtypeStruct((CHIPS, TOKEN_PART, HEAD), bf16),
            jax.ShapeDtypeStruct((HEADS_HERE, 2, CORES * TEXT_CORE, HEAD), bf16),
        ],
        scratch_shapes=[pltpu.VMEM((CHIPS * 2 * TEXT_HERE, HEAD), f32)],
        compiler_params=params(14),
        cost_estimate=pl.CostEstimate(
            flops=400_000_000, bytes_accessed=3_000_000, transcendentals=1_200_000
        ),
        name="temporal",
    )(info, rows, text_own, text_other)


FRAME_KEYS = 2 * ROWS
VIDEO_KEYS = 2 * FRAME_KEYS
ALL_KEYS = VIDEO_KEYS + CORES * TEXT_CORE


def spatial_kernel(info, own, partner, *refs):
    firsts, (text_ref, out_ref, keys, values) = refs[: 2 * Y], refs[2 * Y :]
    core, length, frame = info[3], info[4], info[5]
    shift = jnp.where(frame == 0, -MASKED, 0.0).astype(f32)
    step = 256
    count = step // PIECE
    for h in range(HEADS_HERE):
        part = slice(h * PIECE, (h + 1) * PIECE)
        head_lanes = slice(h * HEAD, (h + 1) * HEAD)

        @pl.when(info[h] != 0)
        def _():
            place = 0
            for ref in (own, partner, *firsts):
                rows = ref.shape[0] * PIECE
                width = ref.shape[2]
                block = ref[:, part, width - 2 * HEAD :].reshape(rows, 2 * HEAD)
                keys[place : place + rows, :] = block[:, :HEAD]
                values[place : place + rows, :] = block[:, HEAD:]
                place += rows
            keys[VIDEO_KEYS:, :] = text_ref[h, 0]
            values[VIDEO_KEYS:, :] = text_ref[h, 1]

            def body(index, _):
                query = own[pl.ds(index * count, count), part, :HEAD].reshape(step, HEAD)
                here = nt(query, keys[:FRAME_KEYS, :])
                first = nt(query, keys[FRAME_KEYS:VIDEO_KEYS, :])
                text = mask_text(nt(query, keys[VIDEO_KEYS:, :]), core, length)
                top = FACTOR * functools.reduce(
                    jnp.maximum, [jnp.max(s, axis=1, keepdims=True) for s in (here, first, text)]
                )
                total, summed = weigh(here, top, values[:FRAME_KEYS, :], 0.0, 0.0)
                total, summed = weigh(
                    first, top + shift, values[FRAME_KEYS:VIDEO_KEYS, :], total, summed
                )
                total, summed = weigh(text, top, values[VIDEO_KEYS:, :], total, summed)
                rows = pl.ds(pl.multiple_of(index * step, step), step)
                out_ref[rows, head_lanes] = (summed / total).astype(bf16)
                return 0

            lax.fori_loop(0, ROWS // step, body, 0)


def spatial(info, own, partner, firsts, text):
    return pl.pallas_call(
        spatial_kernel,
        in_specs=specs(3 + 2 * Y),
        out_specs=pl.BlockSpec(memory_space=pltpu.VMEM),
        out_shape=jax.ShapeDtypeStruct((ROWS, TRIPLE), bf16),
        scratch_shapes=[pltpu.VMEM((ALL_KEYS, HEAD), bf16)] * 2,
        compiler_params=params(20),
        cost_estimate=pl.CostEstimate(
            flops=500_000_000, bytes_accessed=1_000_000, transcendentals=0
        ),
        name="spatial",
    )(info, own, partner, *firsts, text)


def merge_kernel(info, spatial_ref, back, *outs):
    plane = info[6]
    count = CHIPS // PLANES
    for index in range(PLANES):
        step = (index - plane) & (PLANES - 1)
        for k, out_ref in enumerate(outs):

            @pl.when(step == k)
            def _():
                out_ref[...] = spatial_ref[index * BLOCK : (index + 1) * BLOCK, :]
                for h in range(HEADS_HERE):

                    @pl.when(info[h] == 0)
                    def _():
                        rows = back[
                            index * count : (index + 1) * count, h * PIECE : (h + 1) * PIECE, :
                        ]
                        out_ref[:, h * HEAD : (h + 1) * HEAD] = rows.reshape(BLOCK, HEAD)


def merge(info, over_space, back):
    return pl.pallas_call(
        merge_kernel,
        in_specs=specs(2),
        out_specs=[pl.BlockSpec(memory_space=pltpu.VMEM)] * PLANES,
        out_shape=[jax.ShapeDtypeStruct((BLOCK, TRIPLE), bf16)] * PLANES,
        compiler_params=params(4),
        name="merge",
    )(info, over_space, back)


def out_kernel(place, *refs):
    rows, own, mine, theirs, out_ref = refs[:4], refs[4], refs[5:8], refs[8:11], refs[11]
    core = place[3]
    wide = WIDTH // CORES
    for which in range(CORES):
        for side, weights in ((which, mine), (1 - which, theirs)):
            lanes = slice(side * wide, (side + 1) * wide)

            @pl.when(core == which)
            def _():
                total = jnp.dot(rows[0][...], own[:, lanes], preferred_element_type=f32)
                for k in range(3):
                    total += jnp.dot(rows[k + 1][...], weights[k][...], preferred_element_type=f32)
                out_ref[:, lanes] = total.astype(bf16)


def out_project(info, rows, own, mine, theirs):
    return pl.pallas_call(
        out_kernel,
        in_specs=specs(11),
        out_specs=pl.BlockSpec(memory_space=pltpu.VMEM),
        out_shape=jax.ShapeDtypeStruct((BLOCK, WIDTH), bf16),
        compiler_params=params(12),
        cost_estimate=pl.CostEstimate(
            flops=2 * BLOCK * 1536 * WIDTH, bytes_accessed=10_500_000, transcendentals=0
        ),
        name="out_project",
    )(info, *rows, own, *mine, *theirs)


def swap_cores(value):
    return lax.ppermute(value, "core", [(0, 1), (1, 0)])


def shifted(value, axis, count, k):
    return lax.ppermute(value, axis, [(i, (i + k) % count) for i in range(count)])


def local(video_tokens, text_tokens, project_in, project_out, head_class, text_length):
    z, y = lax.axis_index("z"), lax.axis_index("y")
    core, plane = lax.axis_index("core"), lax.axis_index("head")
    here = lax.dynamic_slice_in_dim(head_class, plane * HEADS_HERE, HEADS_HERE)
    info = jnp.concatenate([here, jnp.stack([core, text_length[0], z * Y + y, plane])])

    own_out = project_out.reshape(TRIPLE, WIDTH)
    half_out = lax.dynamic_slice_in_dim(own_out, core * (WIDTH // CORES), WIDTH // CORES, 1)
    mine = [shifted(half_out, "head", PLANES, k) for k in (1, 2, 3)]

    weights = jnp.transpose(project_in, (1, 0, 2))
    packed = project(video_tokens, text_tokens, weights)
    moved = lax.all_to_all(packed, ("z", "y"), 0, 0, tiled=True)
    partner = swap_cores(packed)

    text_own = moved[:, TOKEN_PART:, :]
    text_other = swap_cores(text_own)

    first_piece = moved[0, :TOKEN_PART, HEAD:]
    copies = jnp.broadcast_to(first_piece[None], (Z,) + first_piece.shape)
    column = lax.all_to_all(copies, "z", 0, 0, tiled=True)
    over_time, text = temporal(info, moved, text_own, text_other)
    column, over_time = lax.optimization_barrier((column, over_time))
    back = lax.all_to_all(over_time, ("z", "y"), 0, 0, tiled=True)
    columns = [column] + [shifted(column, "y", Y, k) for k in range(1, Y)]
    firsts = columns + [swap_cores(c) for c in columns]

    over_space = spatial(info, packed, partner, firsts, text)
    mine, over_space, back = lax.optimization_barrier((mine, over_space, back))
    theirs = [swap_cores(m) for m in mine]
    parts = merge(info, over_space, back)
    gathered = [parts[0]] + [shifted(parts[k], "head", PLANES, k) for k in (1, 2, 3)]
    return out_project(info, gathered, own_out, mine, theirs)


def solution(mesh):
    split = Mesh(mesh.devices.reshape(Z, Y, CORES, PLANES), ("z", "y", "core", "head"))
    seq = ("z", "y", "core")
    placed = (
        P(seq, None),
        P(seq, None),
        P(None, "head", None),
        P("head", None, None),
        P(),
        P(),
    )
    return jax.shard_map(
        local, mesh=split, in_specs=placed, out_specs=P(seq + ("head",), None), check_vma=False
    )
```

```python
import functools
import math

import jax
import jax.numpy as jnp
from jax import lax
from jax.experimental import pallas as pl
from jax.experimental.pallas import tpu as pltpu
from jax.sharding import Mesh, PartitionSpec as P

Z, Y, CORES, PLANES = 8, 4, 2, 4
CHIPS = Z * Y
HEADS_HERE = 3
HEAD = 128
TRIPLE = 3 * HEAD
ROWS = 512
BLOCK = ROWS // PLANES
PIECE = ROWS // CHIPS
TEXT_HERE = 4
TEXT_CORE = CHIPS * TEXT_HERE
TOKEN_PART = HEADS_HERE * PIECE
CHUNK = TOKEN_PART + 2 * TEXT_HERE
WIDTH = 3072
MASKED = -1e30
FACTOR = HEAD**-0.5 * math.log2(math.e)
MIB = 1024 * 1024

f32 = jnp.float32
bf16 = jnp.bfloat16


def params(mib):
    return pltpu.CompilerParams(vmem_limit_bytes=mib * MIB)


def nt(a, b):
    return lax.dot_general(a, b, (((1,), (1,)), ((), ())), preferred_element_type=f32)


CUTS = ((0, 1536), (1536, 1536))
TALL = ROWS + 16


def project_kernel(x_hbm, text_ref, w_hbm, out_ref, x, w, total, text_rows, x_sem, w_sem):

    def fetch(part):
        depth = pl.ds(*CUTS[part])
        yield pltpu.make_async_copy(x_hbm.at[:, depth], x.at[pl.ds(0, ROWS), depth], x_sem.at[part])
        for h in range(HEADS_HERE):
            lanes = pl.ds(h * TRIPLE, TRIPLE)
            yield pltpu.make_async_copy(
                w_hbm.at[h, depth], w.at[depth, lanes], w_sem.at[part, h]
            )

    for part in range(len(CUTS)):
        for copy in fetch(part):
            copy.start()
    padding = jnp.zeros((TALL - ROWS - TEXT_HERE, WIDTH), f32)
    x[ROWS:, :] = jnp.concatenate([text_ref[...].astype(f32), padding], axis=0).astype(bf16)

    blocks = ((0, 256), (256, TALL))
    for part, (first, depth) in enumerate(CUTS):
        for copy in fetch(part):
            copy.wait()
        for start, stop in blocks:
            partial = jnp.dot(
                x[start:stop, first : first + depth],
                w[first : first + depth, :],
                preferred_element_type=f32,
            )
            if part == 0:
                total[start:stop, :] = partial
                continue
            rows = total[start:stop, :] + partial
            tokens = min(stop, ROWS) - start
            chips = slice(start // PIECE, (start + tokens) // PIECE)
            for h in range(HEADS_HERE):
                piece = rows[:tokens, h * TRIPLE : (h + 1) * TRIPLE].astype(bf16)
                out_ref[chips, h * PIECE : (h + 1) * PIECE, :] = piece.reshape(
                    tokens // PIECE, PIECE, TRIPLE
                )
    for h in range(HEADS_HERE):
        text = rows[tokens : tokens + 8, h * TRIPLE : (h + 1) * TRIPLE]
        lanes = slice(h * HEAD, (h + 1) * HEAD)
        text_rows[0:TEXT_HERE, lanes] = text[0:TEXT_HERE, HEAD : 2 * HEAD]
        text_rows[TEXT_HERE : 2 * TEXT_HERE, lanes] = text[0:TEXT_HERE, 2 * HEAD :]
    out_ref[:, TOKEN_PART:, :] = jnp.broadcast_to(
        text_rows[...].astype(bf16)[None], (CHIPS, 2 * TEXT_HERE, TRIPLE)
    )


def project(video_tokens, text_tokens, weights):
    vmem = pl.BlockSpec(memory_space=pltpu.VMEM)
    hbm = pl.BlockSpec(memory_space=pltpu.HBM)
    return pl.pallas_call(
        project_kernel,
        in_specs=[hbm, vmem, hbm],
        out_specs=vmem,
        out_shape=jax.ShapeDtypeStruct((CHIPS, CHUNK, TRIPLE), bf16),
        scratch_shapes=[
            pltpu.VMEM((TALL, WIDTH), bf16),
            pltpu.VMEM((WIDTH, HEADS_HERE * TRIPLE), bf16),
            pltpu.VMEM((TALL, HEADS_HERE * TRIPLE), f32),
            pltpu.VMEM((2 * TEXT_HERE, TRIPLE), f32),
            pltpu.SemaphoreType.DMA((len(CUTS),)),
            pltpu.SemaphoreType.DMA((len(CUTS), HEADS_HERE)),
        ],
        compiler_params=params(62),
        cost_estimate=pl.CostEstimate(
            flops=2 * ROWS * WIDTH * 3 * TRIPLE, bytes_accessed=12_000_000, transcendentals=0
        ),
        name="project",
    )(video_tokens, text_tokens, weights)


def text_slots(rows, core):
    row = lax.broadcasted_iota(jnp.int32, (rows, TEXT_CORE), 1)
    chip = row & (CHIPS - 1)
    return chip * (CORES * TEXT_HERE) + core * TEXT_HERE + lax.shift_right_logical(row, 5)


def weigh(scores, top, values, total, summed):
    weights = jnp.exp2(scores * FACTOR - top)
    total = total + jnp.sum(weights, axis=1, keepdims=True)
    summed = summed + jnp.dot(weights.astype(bf16), values, preferred_element_type=f32)
    return total, summed


def mask_text(scores, core, length):
    slots = jnp.concatenate(
        [text_slots(scores.shape[0], core), text_slots(scores.shape[0], 1 - core)], axis=1
    )
    return jnp.where(slots < length, scores, MASKED)


def temporal_kernel(info, rows_ref, text_own, text_other, out_ref, text_ref, spread):
    core, length = info[3], info[4]

    for side, source in enumerate((text_own, text_other)):
        for h in range(HEADS_HERE):
            lanes = source[:, :, h * HEAD : (h + 1) * HEAD].astype(f32)
            spread[...] = lanes.reshape(CHIPS * 2 * TEXT_HERE, HEAD)
            for kind in range(2):
                for t in range(TEXT_HERE):
                    rows = pl.ds(kind * TEXT_HERE + t, CHIPS, stride=2 * TEXT_HERE)
                    first = side * TEXT_CORE + t * CHIPS
                    text_ref[h, kind, first : first + CHIPS, :] = spread[rows, :].astype(bf16)

    step = 128
    count = step // PIECE
    for h in range(HEADS_HERE):
        part = slice(h * PIECE, (h + 1) * PIECE)

        @pl.when(info[h] == 0)
        def _():
            keys = rows_ref[:, part, HEAD : 2 * HEAD].reshape(ROWS, HEAD)
            values = rows_ref[:, part, 2 * HEAD :].reshape(ROWS, HEAD)
            for index in range(ROWS // step):
                chips = slice(index * count, (index + 1) * count)
                query = rows_ref[chips, part, :HEAD].reshape(step, HEAD)
                scores = nt(query, keys)
                own = lax.broadcasted_iota(jnp.int32, scores.shape, 0) & (PIECE - 1)
                other = lax.broadcasted_iota(jnp.int32, scores.shape, 1) & (PIECE - 1)
                scores = jnp.where(own == other, scores, MASKED)
                text = mask_text(nt(query, text_ref[h, 0]), core, length)
                top = FACTOR * jnp.maximum(
                    jnp.max(scores, axis=1, keepdims=True), jnp.max(text, axis=1, keepdims=True)
                )
                total, summed = weigh(scores, top, values, 0.0, 0.0)
                total, summed = weigh(text, top, text_ref[h, 1], total, summed)
                result = (summed / total).astype(bf16)
                out_ref[chips, part, :] = result.reshape(count, PIECE, HEAD)

        @pl.when(info[h] != 0)
        def _():
            out_ref[:, part, :] = jnp.zeros((CHIPS, PIECE, HEAD), bf16)


def specs(count):
    return [pl.BlockSpec(memory_space=pltpu.SMEM)] + [
        pl.BlockSpec(memory_space=pltpu.VMEM)
    ] * count


def temporal(info, rows, text_own, text_other):
    return pl.pallas_call(
        temporal_kernel,
        in_specs=specs(3),
        out_specs=[pl.BlockSpec()] * 2,
        out_shape=[
            pltpu.HBM((CHIPS, TOKEN_PART, HEAD), bf16),
            pltpu.HBM((HEADS_HERE, 2, CORES * TEXT_CORE, HEAD), bf16),
        ],
        scratch_shapes=[pltpu.VMEM((CHIPS * 2 * TEXT_HERE, HEAD), f32)],
        compiler_params=params(14),
        cost_estimate=pl.CostEstimate(
            flops=400_000_000, bytes_accessed=3_000_000, transcendentals=1_200_000
        ),
        name="temporal",
    )(info, rows, text_own, text_other)


FRAME_KEYS = 2 * ROWS
VIDEO_KEYS = 2 * FRAME_KEYS
ALL_KEYS = VIDEO_KEYS + CORES * TEXT_CORE


def spatial_kernel(info, own, partner, *refs):
    firsts, (text_ref, out_ref, keys, values) = refs[: 2 * Y], refs[2 * Y :]
    core, length, frame = info[3], info[4], info[5]
    shift = jnp.where(frame == 0, -MASKED, 0.0).astype(f32)
    step = 256
    count = step // PIECE
    for h in range(HEADS_HERE):
        part = slice(h * PIECE, (h + 1) * PIECE)
        head_lanes = slice(h * HEAD, (h + 1) * HEAD)

        @pl.when(info[h] != 0)
        def _():
            place = 0
            for ref in (own, partner, *firsts):
                rows = ref.shape[0] * PIECE
                width = ref.shape[2]
                block = ref[:, part, width - 2 * HEAD :].reshape(rows, 2 * HEAD)
                keys[place : place + rows, :] = block[:, :HEAD]
                values[place : place + rows, :] = block[:, HEAD:]
                place += rows
            keys[VIDEO_KEYS:, :] = text_ref[h, 0]
            values[VIDEO_KEYS:, :] = text_ref[h, 1]

            def body(index, _):
                query = own[pl.ds(index * count, count), part, :HEAD].reshape(step, HEAD)
                here = nt(query, keys[:FRAME_KEYS, :])
                first = nt(query, keys[FRAME_KEYS:VIDEO_KEYS, :])
                text = mask_text(nt(query, keys[VIDEO_KEYS:, :]), core, length)
                top = FACTOR * functools.reduce(
                    jnp.maximum, [jnp.max(s, axis=1, keepdims=True) for s in (here, first, text)]
                )
                total, summed = weigh(here, top, values[:FRAME_KEYS, :], 0.0, 0.0)
                total, summed = weigh(
                    first, top + shift, values[FRAME_KEYS:VIDEO_KEYS, :], total, summed
                )
                total, summed = weigh(text, top, values[VIDEO_KEYS:, :], total, summed)
                rows = pl.ds(pl.multiple_of(index * step, step), step)
                out_ref[rows, head_lanes] = (summed / total).astype(bf16)
                return 0

            lax.fori_loop(0, ROWS // step, body, 0)


def spatial(info, own, partner, firsts, text):
    return pl.pallas_call(
        spatial_kernel,
        in_specs=specs(2 + 2 * Y) + [pl.BlockSpec()],
        out_specs=pl.BlockSpec(),
        out_shape=pltpu.HBM((ROWS, TRIPLE), bf16),
        scratch_shapes=[pltpu.VMEM((ALL_KEYS, HEAD), bf16)] * 2,
        compiler_params=params(20),
        cost_estimate=pl.CostEstimate(
            flops=4_000_000_000, bytes_accessed=1_000_000, transcendentals=0
        ),
        name="spatial",
    )(info, own, partner, *firsts, pltpu.with_memory_space_constraint(text, pltpu.HBM))


def merge_kernel(info, spatial_ref, back, *outs):
    plane = info[6]
    count = CHIPS // PLANES
    for index in range(PLANES):
        step = (index - plane) & (PLANES - 1)
        for k, out_ref in enumerate(outs):

            @pl.when(step == k)
            def _():
                out_ref[...] = spatial_ref[index * BLOCK : (index + 1) * BLOCK, :]
                for h in range(HEADS_HERE):

                    @pl.when(info[h] == 0)
                    def _():
                        rows = back[
                            index * count : (index + 1) * count, h * PIECE : (h + 1) * PIECE, :
                        ]
                        out_ref[:, h * HEAD : (h + 1) * HEAD] = rows.reshape(BLOCK, HEAD)


def merge(info, over_space, back):
    return pl.pallas_call(
        merge_kernel,
        in_specs=specs(0) + [pl.BlockSpec()] + specs(1)[1:],
        out_specs=[pl.BlockSpec(memory_space=pltpu.VMEM)] * PLANES,
        out_shape=[jax.ShapeDtypeStruct((BLOCK, TRIPLE), bf16)] * PLANES,
        compiler_params=params(4),
        name="merge",
    )(info, pltpu.with_memory_space_constraint(over_space, pltpu.HBM), back)


QUARTER = WIDTH // CORES // 2
FAR = PLANES - 1


def hold_kernel(*refs):
    sources, held, sem = refs[: 4 * FAR], refs[4 * FAR], refs[4 * FAR + 1]
    copies = [
        pltpu.make_async_copy(
            source, held.at[n // (2 * FAR) * 2 + n % 2, n % (2 * FAR) // 2], sem.at[n]
        )
        for n, source in enumerate(sources)
    ]
    for copy in copies:
        copy.start()
    for copy in copies:
        copy.wait()


def hold(weights):
    shape = (4, FAR, TRIPLE, QUARTER)
    return pl.pallas_call(
        hold_kernel,
        in_specs=[pl.BlockSpec(memory_space=pltpu.HBM)] * len(weights),
        out_specs=pl.BlockSpec(memory_space=pltpu.VMEM),
        out_shape=pltpu.VMEM(shape, bf16),
        scratch_shapes=[pltpu.SemaphoreType.DMA((4 * FAR,))],
        compiler_params=params(4),
        cost_estimate=pl.CostEstimate(
            flops=1_000_000, bytes_accessed=7_000_000, transcendentals=0
        ),
        name="hold",
    )(*[pltpu.with_memory_space_constraint(w, pltpu.HBM) for w in weights])


def out_kernel(info, r0, r1, r2, r3, own, held, out_ref):
    core = info[3]
    for which in range(CORES):

        @pl.when(core == which)
        def _():
            for q in range(4):
                first = ((which + q // 2) % CORES * 2 + q % 2) * QUARTER
                lanes = slice(first, first + QUARTER)
                total = jnp.dot(r0[...], own[:, lanes], preferred_element_type=f32)
                for k, rows in enumerate((r1, r2, r3)):
                    total += jnp.dot(rows[...], held[q, k], preferred_element_type=f32)
                out_ref[:, lanes] = total.astype(bf16)


def out_project(info, rows, own, held):
    return pl.pallas_call(
        out_kernel,
        in_specs=specs(6),
        out_specs=pl.BlockSpec(memory_space=pltpu.VMEM),
        out_shape=jax.ShapeDtypeStruct((BLOCK, WIDTH), bf16),
        compiler_params=params(8),
        cost_estimate=pl.CostEstimate(
            flops=2 * BLOCK * 1536 * WIDTH, bytes_accessed=10_500_000, transcendentals=0
        ),
        name="out_project",
    )(info, *rows, own, held)


def swap_cores(value):
    return lax.ppermute(value, "core", [(0, 1), (1, 0)])


def shifted(value, axis, count, k):
    return lax.ppermute(value, axis, [(i, (i + k) % count) for i in range(count)])


def local(video_tokens, text_tokens, project_in, project_out, head_class, text_length):
    z, y = lax.axis_index("z"), lax.axis_index("y")
    core, plane = lax.axis_index("core"), lax.axis_index("head")
    here = lax.dynamic_slice_in_dim(head_class, plane * HEADS_HERE, HEADS_HERE)
    info = jnp.concatenate([here, jnp.stack([core, text_length[0], z * Y + y, plane])])

    own_out = project_out.reshape(TRIPLE, WIDTH)
    wide = WIDTH // CORES // 2
    pieces = [
        lax.dynamic_slice_in_dim(own_out, (2 * core + part) * wide, wide, 1) for part in range(2)
    ]

    weights = jnp.transpose(project_in, (1, 0, 2))
    packed = project(video_tokens, text_tokens, weights)
    moved = lax.all_to_all(packed, ("z", "y"), 0, 0, tiled=True)
    partner = swap_cores(packed)

    right = [shifted(p, "head", PLANES, 1) for p in pieces]
    left = [shifted(p, "head", PLANES, PLANES - 1) for p in pieces]
    first_swap = [swap_cores(m) for m in right]
    moved, partner, left, first_swap = lax.optimization_barrier((moved, partner, left, first_swap))
    later_swap = [swap_cores(m) for m in left]
    across = [
        shifted(right[0], "head", PLANES, 1),
        shifted(left[1], "head", PLANES, PLANES - 1),
    ]

    first_piece = moved[0, :TOKEN_PART, HEAD:]
    copies = jnp.broadcast_to(first_piece[None], (Z,) + first_piece.shape)
    column = lax.all_to_all(copies, "z", 0, 0, tiled=True)
    text_own = moved[:, TOKEN_PART:, :]
    text_other = swap_cores(text_own)
    over_time, text = temporal(info, moved, text_own, text_other)
    column, over_time, later_swap = lax.optimization_barrier((column, over_time, later_swap))
    theirs = first_swap + later_swap
    back = lax.all_to_all(over_time, ("z", "y"), 0, 0, tiled=True)
    columns = [column] + [shifted(column, "y", Y, k) for k in range(1, Y)]
    firsts = columns + [swap_cores(c) for c in columns]

    over_space = spatial(info, packed, partner, firsts, text)
    parts = merge(info, over_space, back)
    mine = right + left + across
    theirs = theirs + [swap_cores(a) for a in across]
    held = hold(mine + theirs)
    gathered = [parts[0]] + [shifted(parts[k], "head", PLANES, k) for k in (1, 3, 2)]
    return out_project(info, gathered, own_out, held)


def solution(mesh):
    split = Mesh(mesh.devices.reshape(Z, Y, CORES, PLANES), ("z", "y", "core", "head"))
    seq = ("z", "y", "core")
    placed = (
        P(seq, None),
        P(seq, None),
        P(None, "head", None),
        P("head", None, None),
        P(),
        P(),
    )
    return jax.shard_map(
        local, mesh=split, in_specs=placed, out_specs=P(seq + ("head",), None), check_vma=False
    )
```

```python
import functools
import math

import jax
import jax.numpy as jnp
from jax import lax
from jax.experimental import pallas as pl
from jax.experimental.pallas import tpu as pltpu
from jax.sharding import Mesh, PartitionSpec as P

Z, Y, CORES, PLANES = 8, 4, 2, 4
CHIPS = Z * Y
HEADS_HERE = 3
HEAD = 128
TRIPLE = 3 * HEAD
ROWS = 512
BLOCK = ROWS // PLANES
PIECE = ROWS // CHIPS
TEXT_HERE = 4
TEXT_CORE = CHIPS * TEXT_HERE
TOKEN_PART = HEADS_HERE * PIECE
CHUNK = TOKEN_PART + 2 * TEXT_HERE
WIDTH = 3072
MASKED = -1e30
FACTOR = HEAD**-0.5 * math.log2(math.e)
MIB = 1024 * 1024

f32 = jnp.float32
bf16 = jnp.bfloat16


def params(mib):
    return pltpu.CompilerParams(vmem_limit_bytes=mib * MIB)


def nt(a, b):
    return lax.dot_general(a, b, (((1,), (1,)), ((), ())), preferred_element_type=f32)


CUTS = ((0, 1536), (1536, 1536))
TALL = ROWS + 16


def project_kernel(x_hbm, text_ref, w_hbm, out_ref, x, w, total, text_rows, x_sem, w_sem):

    def fetch(part):
        depth = pl.ds(*CUTS[part])
        yield pltpu.make_async_copy(x_hbm.at[:, depth], x.at[pl.ds(0, ROWS), depth], x_sem.at[part])
        for h in range(HEADS_HERE):
            lanes = pl.ds(h * TRIPLE, TRIPLE)
            yield pltpu.make_async_copy(
                w_hbm.at[h, depth], w.at[depth, lanes], w_sem.at[part, h]
            )

    for part in range(len(CUTS)):
        for copy in fetch(part):
            copy.start()
    padding = jnp.zeros((TALL - ROWS - TEXT_HERE, WIDTH), f32)
    x[ROWS:, :] = jnp.concatenate([text_ref[...].astype(f32), padding], axis=0).astype(bf16)

    blocks = ((0, 256), (256, TALL))
    for part, (first, depth) in enumerate(CUTS):
        for copy in fetch(part):
            copy.wait()
        for start, stop in blocks:
            partial = jnp.dot(
                x[start:stop, first : first + depth],
                w[first : first + depth, :],
                preferred_element_type=f32,
            )
            if part == 0:
                total[start:stop, :] = partial
                continue
            rows = total[start:stop, :] + partial
            tokens = min(stop, ROWS) - start
            chips = slice(start // PIECE, (start + tokens) // PIECE)
            for h in range(HEADS_HERE):
                piece = rows[:tokens, h * TRIPLE : (h + 1) * TRIPLE].astype(bf16)
                out_ref[chips, h * PIECE : (h + 1) * PIECE, :] = piece.reshape(
                    tokens // PIECE, PIECE, TRIPLE
                )
    for h in range(HEADS_HERE):
        text = rows[tokens : tokens + 8, h * TRIPLE : (h + 1) * TRIPLE]
        lanes = slice(h * HEAD, (h + 1) * HEAD)
        text_rows[0:TEXT_HERE, lanes] = text[0:TEXT_HERE, HEAD : 2 * HEAD]
        text_rows[TEXT_HERE : 2 * TEXT_HERE, lanes] = text[0:TEXT_HERE, 2 * HEAD :]
    out_ref[:, TOKEN_PART:, :] = jnp.broadcast_to(
        text_rows[...].astype(bf16)[None], (CHIPS, 2 * TEXT_HERE, TRIPLE)
    )


def project(video_tokens, text_tokens, weights):
    vmem = pl.BlockSpec(memory_space=pltpu.VMEM)
    hbm = pl.BlockSpec(memory_space=pltpu.HBM)
    return pl.pallas_call(
        project_kernel,
        in_specs=[hbm, vmem, hbm],
        out_specs=vmem,
        out_shape=jax.ShapeDtypeStruct((CHIPS, CHUNK, TRIPLE), bf16),
        scratch_shapes=[
            pltpu.VMEM((TALL, WIDTH), bf16),
            pltpu.VMEM((WIDTH, HEADS_HERE * TRIPLE), bf16),
            pltpu.VMEM((TALL, HEADS_HERE * TRIPLE), f32),
            pltpu.VMEM((2 * TEXT_HERE, TRIPLE), f32),
            pltpu.SemaphoreType.DMA((len(CUTS),)),
            pltpu.SemaphoreType.DMA((len(CUTS), HEADS_HERE)),
        ],
        compiler_params=params(62),
        cost_estimate=pl.CostEstimate(
            flops=2 * ROWS * WIDTH * 3 * TRIPLE, bytes_accessed=12_000_000, transcendentals=0
        ),
        name="project",
    )(video_tokens, text_tokens, weights)


def text_slots(rows, core):
    row = lax.broadcasted_iota(jnp.int32, (rows, TEXT_CORE), 1)
    chip = row & (CHIPS - 1)
    return chip * (CORES * TEXT_HERE) + core * TEXT_HERE + lax.shift_right_logical(row, 5)


def weigh(scores, top, values, total, summed):
    weights = jnp.exp2(scores * FACTOR - top)
    total = total + jnp.sum(weights, axis=1, keepdims=True)
    summed = summed + jnp.dot(weights.astype(bf16), values, preferred_element_type=f32)
    return total, summed


def mask_text(scores, core, length):
    slots = jnp.concatenate(
        [text_slots(scores.shape[0], core), text_slots(scores.shape[0], 1 - core)], axis=1
    )
    return jnp.where(slots < length, scores, MASKED)


def temporal_kernel(info, rows_ref, text_own, text_other, out_ref, text_ref, spread):
    core, length = info[3], info[4]

    for side, source in enumerate((text_own, text_other)):
        for h in range(HEADS_HERE):
            lanes = source[:, :, h * HEAD : (h + 1) * HEAD].astype(f32)
            spread[: CHIPS * 2 * TEXT_HERE, :] = lanes.reshape(CHIPS * 2 * TEXT_HERE, HEAD)
            for kind in range(2):
                for t in range(TEXT_HERE):
                    rows = pl.ds(kind * TEXT_HERE + t, CHIPS, stride=2 * TEXT_HERE)
                    first = side * TEXT_CORE + t * CHIPS
                    text_ref[h, kind, first : first + CHIPS, :] = spread[rows, :].astype(bf16)

    step = 128
    count = step // PIECE
    for h in range(HEADS_HERE):
        part = slice(h * PIECE, (h + 1) * PIECE)

        @pl.when(info[h] == 0)
        def _():
            keys = rows_ref[:, part, HEAD : 2 * HEAD].reshape(ROWS, HEAD)
            values = rows_ref[:, part, 2 * HEAD :].reshape(ROWS, HEAD)
            for index in range(ROWS // step):
                chips = slice(index * count, (index + 1) * count)
                query = rows_ref[chips, part, :HEAD].reshape(step, HEAD)
                scores = nt(query, keys)
                own = lax.broadcasted_iota(jnp.int32, scores.shape, 0) & (PIECE - 1)
                other = lax.broadcasted_iota(jnp.int32, scores.shape, 1) & (PIECE - 1)
                scores = jnp.where(own == other, scores, MASKED)
                text = mask_text(nt(query, text_ref[h, 0]), core, length)
                top = FACTOR * jnp.maximum(
                    jnp.max(scores, axis=1, keepdims=True), jnp.max(text, axis=1, keepdims=True)
                )
                total, summed = weigh(scores, top, values, 0.0, 0.0)
                total, summed = weigh(text, top, text_ref[h, 1], total, summed)
                result = (summed / total).astype(bf16)
                out_ref[chips, part, :] = result.reshape(count, PIECE, HEAD)

        @pl.when(info[h] != 0)
        def _():
            out_ref[:, part, :] = jnp.zeros((CHIPS, PIECE, HEAD), bf16)


def specs(count):
    return [pl.BlockSpec(memory_space=pltpu.SMEM)] + [
        pl.BlockSpec(memory_space=pltpu.VMEM)
    ] * count


def temporal(info, rows, text_own, text_other):
    return pl.pallas_call(
        temporal_kernel,
        in_specs=specs(3),
        out_specs=[pl.BlockSpec()] * 2,
        out_shape=[
            pltpu.HBM((CHIPS, TOKEN_PART, HEAD), bf16),
            pltpu.HBM((HEADS_HERE, 2, CORES * TEXT_CORE, HEAD), bf16),
        ],
        scratch_shapes=[pltpu.VMEM(((CHIPS + 1) * 2 * TEXT_HERE, HEAD), f32)],
        compiler_params=params(14),
        cost_estimate=pl.CostEstimate(
            flops=400_000_000, bytes_accessed=3_000_000, transcendentals=1_200_000
        ),
        name="temporal",
    )(info, rows, text_own, text_other)


FRAME_KEYS = 2 * ROWS
VIDEO_KEYS = 2 * FRAME_KEYS
ALL_KEYS = VIDEO_KEYS + CORES * TEXT_CORE


def spatial_kernel(info, own, partner, *refs):
    firsts, (text_ref, out_ref, keys, values) = refs[: 2 * Y], refs[2 * Y :]
    core, length, frame = info[3], info[4], info[5]
    shift = jnp.where(frame == 0, -MASKED, 0.0).astype(f32)
    step = 256
    count = step // PIECE
    for h in range(HEADS_HERE):
        part = slice(h * PIECE, (h + 1) * PIECE)
        head_lanes = slice(h * HEAD, (h + 1) * HEAD)

        @pl.when(info[h] != 0)
        def _():
            place = 0
            for ref in (own, partner, *firsts):
                rows = ref.shape[0] * PIECE
                width = ref.shape[2]
                block = ref[:, part, width - 2 * HEAD :].reshape(rows, 2 * HEAD)
                keys[place : place + rows, :] = block[:, :HEAD]
                values[place : place + rows, :] = block[:, HEAD:]
                place += rows
            keys[VIDEO_KEYS:, :] = text_ref[h, 0]
            values[VIDEO_KEYS:, :] = text_ref[h, 1]

            def body(index, _):
                query = own[pl.ds(index * count, count), part, :HEAD].reshape(step, HEAD)
                here = nt(query, keys[:FRAME_KEYS, :])
                first = nt(query, keys[FRAME_KEYS:VIDEO_KEYS, :])
                text = mask_text(nt(query, keys[VIDEO_KEYS:, :]), core, length)
                top = FACTOR * functools.reduce(
                    jnp.maximum, [jnp.max(s, axis=1, keepdims=True) for s in (here, first, text)]
                )
                total, summed = weigh(here, top, values[:FRAME_KEYS, :], 0.0, 0.0)
                total, summed = weigh(
                    first, top + shift, values[FRAME_KEYS:VIDEO_KEYS, :], total, summed
                )
                total, summed = weigh(text, top, values[VIDEO_KEYS:, :], total, summed)
                rows = pl.ds(pl.multiple_of(index * step, step), step)
                out_ref[rows, head_lanes] = (summed / total).astype(bf16)
                return 0

            lax.fori_loop(0, ROWS // step, body, 0)


def spatial(info, own, partner, firsts, text):
    return pl.pallas_call(
        spatial_kernel,
        in_specs=specs(2 + 2 * Y) + [pl.BlockSpec()],
        out_specs=pl.BlockSpec(),
        out_shape=pltpu.HBM((ROWS, TRIPLE), bf16),
        scratch_shapes=[pltpu.VMEM((ALL_KEYS, HEAD), bf16)] * 2,
        compiler_params=params(20),
        cost_estimate=pl.CostEstimate(
            flops=4_000_000_000, bytes_accessed=1_000_000, transcendentals=0
        ),
        name="spatial",
    )(info, own, partner, *firsts, pltpu.with_memory_space_constraint(text, pltpu.HBM))


def merge_kernel(info, spatial_ref, back, *outs):
    plane = info[6]
    count = CHIPS // PLANES
    for index in range(PLANES):
        step = (index - plane) & (PLANES - 1)
        for k, out_ref in enumerate(outs):

            @pl.when(step == k)
            def _():
                out_ref[...] = spatial_ref[index * BLOCK : (index + 1) * BLOCK, :]
                for h in range(HEADS_HERE):

                    @pl.when(info[h] == 0)
                    def _():
                        rows = back[
                            index * count : (index + 1) * count, h * PIECE : (h + 1) * PIECE, :
                        ]
                        out_ref[:, h * HEAD : (h + 1) * HEAD] = rows.reshape(BLOCK, HEAD)


def merge(info, over_space, back):
    return pl.pallas_call(
        merge_kernel,
        in_specs=specs(0) + [pl.BlockSpec()] + specs(1)[1:],
        out_specs=[pl.BlockSpec(memory_space=pltpu.VMEM)] * PLANES,
        out_shape=[jax.ShapeDtypeStruct((BLOCK, TRIPLE), bf16)] * PLANES,
        compiler_params=params(4),
        name="merge",
    )(info, pltpu.with_memory_space_constraint(over_space, pltpu.HBM), back)


QUARTER = WIDTH // CORES // 2
FAR = PLANES - 1


def hold_kernel(*refs):
    sources, held, sem = refs[: 4 * FAR], refs[4 * FAR], refs[4 * FAR + 1]
    copies = [
        pltpu.make_async_copy(
            source, held.at[n // (2 * FAR) * 2 + n % 2, n % (2 * FAR) // 2], sem.at[n]
        )
        for n, source in enumerate(sources)
    ]
    for copy in copies:
        copy.start()
    for copy in copies:
        copy.wait()


def hold(weights):
    shape = (4, FAR, TRIPLE, QUARTER)
    return pl.pallas_call(
        hold_kernel,
        in_specs=[pl.BlockSpec(memory_space=pltpu.HBM)] * len(weights),
        out_specs=pl.BlockSpec(memory_space=pltpu.VMEM),
        out_shape=pltpu.VMEM(shape, bf16),
        scratch_shapes=[pltpu.SemaphoreType.DMA((4 * FAR,))],
        compiler_params=params(4),
        cost_estimate=pl.CostEstimate(
            flops=1_000_000, bytes_accessed=7_000_000, transcendentals=0
        ),
        name="hold",
    )(*[pltpu.with_memory_space_constraint(w, pltpu.HBM) for w in weights])


def out_kernel(info, r0, r1, r2, r3, own, held, out_ref):
    core = info[3]
    for which in range(CORES):

        @pl.when(core == which)
        def _():
            for q in range(4):
                first = ((which + q // 2) % CORES * 2 + q % 2) * QUARTER
                lanes = slice(first, first + QUARTER)
                total = jnp.dot(r0[...], own[:, lanes], preferred_element_type=f32)
                for k, rows in enumerate((r1, r2, r3)):
                    total += jnp.dot(rows[...], held[q, k], preferred_element_type=f32)
                out_ref[:, lanes] = total.astype(bf16)


def out_project(info, rows, own, held):
    return pl.pallas_call(
        out_kernel,
        in_specs=specs(6),
        out_specs=pl.BlockSpec(memory_space=pltpu.VMEM),
        out_shape=jax.ShapeDtypeStruct((BLOCK, WIDTH), bf16),
        compiler_params=params(8),
        cost_estimate=pl.CostEstimate(
            flops=2 * BLOCK * 1536 * WIDTH, bytes_accessed=10_500_000, transcendentals=0
        ),
        name="out_project",
    )(info, *rows, own, held)


def repeat_kernel(rows_hbm, out_ref, piece, sem):
    copy = pltpu.make_async_copy(
        rows_hbm.at[0, pl.ds(0, TOKEN_PART), pl.ds(HEAD, 2 * HEAD)], piece, sem.at[0]
    )
    copy.start()
    copy.wait()
    out_ref[...] = jnp.broadcast_to(piece[...][None], out_ref.shape)


def repeat_first(rows):
    return pl.pallas_call(
        repeat_kernel,
        in_specs=[pl.BlockSpec(memory_space=pltpu.HBM)],
        out_specs=pl.BlockSpec(memory_space=pltpu.VMEM),
        out_shape=jax.ShapeDtypeStruct((Z, TOKEN_PART, 2 * HEAD), bf16),
        scratch_shapes=[
            pltpu.VMEM((TOKEN_PART, 2 * HEAD), bf16),
            pltpu.SemaphoreType.DMA((1,)),
        ],
        compiler_params=params(4),
        cost_estimate=pl.CostEstimate(flops=0, bytes_accessed=300_000, transcendentals=0),
        name="repeat_first",
    )(rows)


def swap_cores(value):
    return lax.ppermute(value, "core", [(0, 1), (1, 0)])


def shifted(value, axis, count, k):
    return lax.ppermute(value, axis, [(i, (i + k) % count) for i in range(count)])


def local(video_tokens, text_tokens, project_in, project_out, head_class, text_length):
    z, y = lax.axis_index("z"), lax.axis_index("y")
    core, plane = lax.axis_index("core"), lax.axis_index("head")
    here = lax.dynamic_slice_in_dim(head_class, plane * HEADS_HERE, HEADS_HERE)
    info = jnp.concatenate([here, jnp.stack([core, text_length[0], z * Y + y, plane])])

    own_out = project_out.reshape(TRIPLE, WIDTH)
    wide = WIDTH // CORES // 2
    pieces = [
        lax.dynamic_slice_in_dim(own_out, (2 * core + part) * wide, wide, 1) for part in range(2)
    ]

    weights = jnp.transpose(project_in, (1, 0, 2))
    packed = project(video_tokens, text_tokens, weights)
    moved = lax.all_to_all(packed, ("z", "y"), 0, 0, tiled=True)
    partner = swap_cores(packed)

    right = [shifted(p, "head", PLANES, 1) for p in pieces]
    left = [shifted(p, "head", PLANES, PLANES - 1) for p in pieces]
    first_swap = [swap_cores(m) for m in right]
    moved, partner, left, first_swap = lax.optimization_barrier((moved, partner, left, first_swap))
    later_swap = [swap_cores(m) for m in left]
    across = [
        shifted(right[0], "head", PLANES, 1),
        shifted(left[1], "head", PLANES, PLANES - 1),
    ]

    column = lax.all_to_all(repeat_first(moved), "z", 0, 0, tiled=True)
    text_own = moved[:, TOKEN_PART:, :]
    text_other = swap_cores(text_own)
    over_time, text = temporal(info, moved, text_own, text_other)
    column, over_time, later_swap = lax.optimization_barrier((column, over_time, later_swap))
    theirs = first_swap + later_swap
    back = lax.all_to_all(over_time, ("z", "y"), 0, 0, tiled=True)
    columns = [column] + [shifted(column, "y", Y, k) for k in range(1, Y)]
    firsts = columns + [swap_cores(c) for c in columns]

    over_space = spatial(info, packed, partner, firsts, text)
    parts = merge(info, over_space, back)
    mine = right + left + across
    theirs = theirs + [swap_cores(a) for a in across]
    held = hold(mine + theirs)
    gathered = [parts[0]] + [shifted(parts[k], "head", PLANES, k) for k in (1, 3, 2)]
    return out_project(info, gathered, own_out, held)


def solution(mesh):
    split = Mesh(mesh.devices.reshape(Z, Y, CORES, PLANES), ("z", "y", "core", "head"))
    seq = ("z", "y", "core")
    placed = (
        P(seq, None),
        P(seq, None),
        P(None, "head", None),
        P("head", None, None),
        P(),
        P(),
    )
    return jax.shard_map(
        local, mesh=split, in_specs=placed, out_specs=P(seq + ("head",), None), check_vma=False
    )
```

```python
import functools
import math

import jax
import jax.numpy as jnp
from jax import lax
from jax.experimental import pallas as pl
from jax.experimental.pallas import tpu as pltpu
from jax.sharding import Mesh, PartitionSpec as P

Z, Y, CORES, PLANES = 8, 4, 2, 4
CHIPS = Z * Y
HEADS_HERE = 3
HEAD = 128
TRIPLE = 3 * HEAD
ROWS = 512
BLOCK = ROWS // PLANES
PIECE = ROWS // CHIPS
TEXT_HERE = 4
TEXT_CORE = CHIPS * TEXT_HERE
TOKEN_PART = HEADS_HERE * PIECE
CHUNK = TOKEN_PART + 2 * TEXT_HERE
WIDTH = 3072
MASKED = -1e30
FACTOR = HEAD**-0.5 * math.log2(math.e)
MIB = 1024 * 1024

f32 = jnp.float32
bf16 = jnp.bfloat16


def params(mib):
    return pltpu.CompilerParams(vmem_limit_bytes=mib * MIB)


def nt(a, b):
    return lax.dot_general(a, b, (((1,), (1,)), ((), ())), preferred_element_type=f32)


CUTS = ((0, 1536), (1536, 1536))
TALL = ROWS + 16


def project_kernel(x_hbm, text_ref, w_hbm, out_ref, x, w, total, text_rows, x_sem, w_sem):

    def fetch(part):
        depth = pl.ds(*CUTS[part])
        yield pltpu.make_async_copy(x_hbm.at[:, depth], x.at[pl.ds(0, ROWS), depth], x_sem.at[part])
        for h in range(HEADS_HERE):
            lanes = pl.ds(h * TRIPLE, TRIPLE)
            yield pltpu.make_async_copy(
                w_hbm.at[h, depth], w.at[depth, lanes], w_sem.at[part, h]
            )

    for part in range(len(CUTS)):
        for copy in fetch(part):
            copy.start()
    padding = jnp.zeros((TALL - ROWS - TEXT_HERE, WIDTH), f32)
    x[ROWS:, :] = jnp.concatenate([text_ref[...].astype(f32), padding], axis=0).astype(bf16)

    blocks = ((0, 256), (256, TALL))
    for part, (first, depth) in enumerate(CUTS):
        for copy in fetch(part):
            copy.wait()
        for start, stop in blocks:
            partial = jnp.dot(
                x[start:stop, first : first + depth],
                w[first : first + depth, :],
                preferred_element_type=f32,
            )
            if part == 0:
                total[start:stop, :] = partial
                continue
            rows = total[start:stop, :] + partial
            tokens = min(stop, ROWS) - start
            chips = slice(start // PIECE, (start + tokens) // PIECE)
            for h in range(HEADS_HERE):
                piece = rows[:tokens, h * TRIPLE : (h + 1) * TRIPLE].astype(bf16)
                out_ref[chips, h * PIECE : (h + 1) * PIECE, :] = piece.reshape(
                    tokens // PIECE, PIECE, TRIPLE
                )
    for h in range(HEADS_HERE):
        text = rows[tokens : tokens + 8, h * TRIPLE : (h + 1) * TRIPLE]
        lanes = slice(h * HEAD, (h + 1) * HEAD)
        text_rows[0:TEXT_HERE, lanes] = text[0:TEXT_HERE, HEAD : 2 * HEAD]
        text_rows[TEXT_HERE : 2 * TEXT_HERE, lanes] = text[0:TEXT_HERE, 2 * HEAD :]
    out_ref[:, TOKEN_PART:, :] = jnp.broadcast_to(
        text_rows[...].astype(bf16)[None], (CHIPS, 2 * TEXT_HERE, TRIPLE)
    )


def project(video_tokens, text_tokens, weights):
    vmem = pl.BlockSpec(memory_space=pltpu.VMEM)
    hbm = pl.BlockSpec(memory_space=pltpu.HBM)
    return pl.pallas_call(
        project_kernel,
        in_specs=[hbm, vmem, hbm],
        out_specs=vmem,
        out_shape=jax.ShapeDtypeStruct((CHIPS, CHUNK, TRIPLE), bf16),
        scratch_shapes=[
            pltpu.VMEM((TALL, WIDTH), bf16),
            pltpu.VMEM((WIDTH, HEADS_HERE * TRIPLE), bf16),
            pltpu.VMEM((TALL, HEADS_HERE * TRIPLE), f32),
            pltpu.VMEM((2 * TEXT_HERE, TRIPLE), f32),
            pltpu.SemaphoreType.DMA((len(CUTS),)),
            pltpu.SemaphoreType.DMA((len(CUTS), HEADS_HERE)),
        ],
        compiler_params=params(62),
        cost_estimate=pl.CostEstimate(
            flops=2 * ROWS * WIDTH * 3 * TRIPLE, bytes_accessed=12_000_000, transcendentals=0
        ),
        name="project",
    )(video_tokens, text_tokens, weights)


def text_slots(rows, core):
    row = lax.broadcasted_iota(jnp.int32, (rows, TEXT_CORE), 1)
    chip = row & (CHIPS - 1)
    return chip * (CORES * TEXT_HERE) + core * TEXT_HERE + lax.shift_right_logical(row, 5)


def weigh(scores, top, values, total, summed):
    weights = jnp.exp2(scores * FACTOR - top)
    total = total + jnp.sum(weights, axis=1, keepdims=True)
    summed = summed + jnp.dot(weights.astype(bf16), values, preferred_element_type=f32)
    return total, summed


def mask_text(scores, core, length):
    slots = jnp.concatenate(
        [text_slots(scores.shape[0], core), text_slots(scores.shape[0], 1 - core)], axis=1
    )
    return jnp.where(slots < length, scores, MASKED)


def temporal_kernel(info, rows_ref, text_own, text_other, out_ref, text_ref, spread, apart):
    core, length = info[3], info[4]

    for side, source in enumerate((text_own, text_other)):
        for h in range(HEADS_HERE):
            lanes = source[:, :, h * HEAD : (h + 1) * HEAD].astype(f32)
            spread[: CHIPS * 2 * TEXT_HERE, :] = lanes.reshape(CHIPS * 2 * TEXT_HERE, HEAD)
            for kind in range(2):
                for t in range(TEXT_HERE):
                    rows = pl.ds(kind * TEXT_HERE + t, CHIPS, stride=2 * TEXT_HERE)
                    first = side * TEXT_CORE + t * CHIPS
                    text_ref[h, kind, first : first + CHIPS, :] = spread[rows, :].astype(bf16)

    step = apart.shape[0]
    count = step // PIECE
    own = lax.broadcasted_iota(jnp.int32, apart.shape, 0) & (PIECE - 1)
    other = lax.broadcasted_iota(jnp.int32, apart.shape, 1) & (PIECE - 1)
    apart[...] = jnp.where(own == other, 0.0, MASKED)
    for h in range(HEADS_HERE):
        part = slice(h * PIECE, (h + 1) * PIECE)

        @pl.when(info[h] == 0)
        def _():
            keys = rows_ref[:, part, HEAD : 2 * HEAD].reshape(ROWS, HEAD)
            values = rows_ref[:, part, 2 * HEAD :].reshape(ROWS, HEAD)
            for index in range(ROWS // step):
                chips = slice(index * count, (index + 1) * count)
                query = rows_ref[chips, part, :HEAD].reshape(step, HEAD)
                scores = nt(query, keys) + apart[...]
                text = mask_text(nt(query, text_ref[h, 0]), core, length)
                top = FACTOR * jnp.maximum(
                    jnp.max(scores, axis=1, keepdims=True), jnp.max(text, axis=1, keepdims=True)
                )
                total, summed = weigh(scores, top, values, 0.0, 0.0)
                total, summed = weigh(text, top, text_ref[h, 1], total, summed)
                result = (summed / total).astype(bf16)
                out_ref[chips, part, :] = result.reshape(count, PIECE, HEAD)

        @pl.when(info[h] != 0)
        def _():
            out_ref[:, part, :] = jnp.zeros((CHIPS, PIECE, HEAD), bf16)


def specs(count):
    return [pl.BlockSpec(memory_space=pltpu.SMEM)] + [
        pl.BlockSpec(memory_space=pltpu.VMEM)
    ] * count


def temporal(info, rows, text_own, text_other):
    return pl.pallas_call(
        temporal_kernel,
        in_specs=specs(3),
        out_specs=[pl.BlockSpec()] * 2,
        out_shape=[
            pltpu.HBM((CHIPS, TOKEN_PART, HEAD), bf16),
            pltpu.HBM((HEADS_HERE, 2, CORES * TEXT_CORE, HEAD), bf16),
        ],
        scratch_shapes=[
            pltpu.VMEM(((CHIPS + 1) * 2 * TEXT_HERE, HEAD), f32),
            pltpu.VMEM((256, ROWS), f32),
        ],
        compiler_params=params(14),
        cost_estimate=pl.CostEstimate(
            flops=400_000_000, bytes_accessed=3_000_000, transcendentals=1_200_000
        ),
        name="temporal",
    )(info, rows, text_own, text_other)


FRAME_KEYS = 2 * ROWS
VIDEO_KEYS = 2 * FRAME_KEYS
ALL_KEYS = VIDEO_KEYS + CORES * TEXT_CORE


def spatial_kernel(info, own, partner, *refs):
    firsts, (text_ref, out_ref, keys, values) = refs[: 2 * Y], refs[2 * Y :]
    core, length, frame = info[3], info[4], info[5]
    shift = jnp.where(frame == 0, -MASKED, 0.0).astype(f32)
    step = 256
    count = step // PIECE
    for h in range(HEADS_HERE):
        part = slice(h * PIECE, (h + 1) * PIECE)
        head_lanes = slice(h * HEAD, (h + 1) * HEAD)

        @pl.when(info[h] != 0)
        def _():
            place = 0
            for ref in (own, partner, *firsts):
                rows = ref.shape[0] * PIECE
                width = ref.shape[2]
                block = ref[:, part, width - 2 * HEAD :].reshape(rows, 2 * HEAD)
                keys[place : place + rows, :] = block[:, :HEAD]
                values[place : place + rows, :] = block[:, HEAD:]
                place += rows
            keys[VIDEO_KEYS:, :] = text_ref[h, 0]
            values[VIDEO_KEYS:, :] = text_ref[h, 1]

            def body(index, _):
                query = own[pl.ds(index * count, count), part, :HEAD].reshape(step, HEAD)
                here = nt(query, keys[:FRAME_KEYS, :])
                first = nt(query, keys[FRAME_KEYS:VIDEO_KEYS, :])
                text = mask_text(nt(query, keys[VIDEO_KEYS:, :]), core, length)
                top = FACTOR * functools.reduce(
                    jnp.maximum, [jnp.max(s, axis=1, keepdims=True) for s in (here, first, text)]
                )
                total, summed = weigh(here, top, values[:FRAME_KEYS, :], 0.0, 0.0)
                total, summed = weigh(
                    first, top + shift, values[FRAME_KEYS:VIDEO_KEYS, :], total, summed
                )
                total, summed = weigh(text, top, values[VIDEO_KEYS:, :], total, summed)
                rows = pl.ds(pl.multiple_of(index * step, step), step)
                out_ref[rows, head_lanes] = (summed / total).astype(bf16)
                return 0

            lax.fori_loop(0, ROWS // step, body, 0)


def spatial(info, own, partner, firsts, text):
    return pl.pallas_call(
        spatial_kernel,
        in_specs=specs(2 + 2 * Y) + [pl.BlockSpec()],
        out_specs=pl.BlockSpec(),
        out_shape=pltpu.HBM((ROWS, TRIPLE), bf16),
        scratch_shapes=[pltpu.VMEM((ALL_KEYS, HEAD), bf16)] * 2,
        compiler_params=params(20),
        cost_estimate=pl.CostEstimate(
            flops=4_000_000_000, bytes_accessed=1_000_000, transcendentals=0
        ),
        name="spatial",
    )(info, own, partner, *firsts, pltpu.with_memory_space_constraint(text, pltpu.HBM))


def merge_kernel(info, spatial_ref, back, *outs):
    plane = info[6]
    count = CHIPS // PLANES
    for index in range(PLANES):
        step = (index - plane) & (PLANES - 1)
        for k, out_ref in enumerate(outs):

            @pl.when(step == k)
            def _():
                out_ref[...] = spatial_ref[index * BLOCK : (index + 1) * BLOCK, :]
                for h in range(HEADS_HERE):

                    @pl.when(info[h] == 0)
                    def _():
                        rows = back[
                            index * count : (index + 1) * count, h * PIECE : (h + 1) * PIECE, :
                        ]
                        out_ref[:, h * HEAD : (h + 1) * HEAD] = rows.reshape(BLOCK, HEAD)


def merge(info, over_space, back):
    return pl.pallas_call(
        merge_kernel,
        in_specs=specs(0) + [pl.BlockSpec()] + specs(1)[1:],
        out_specs=[pl.BlockSpec(memory_space=pltpu.VMEM)] * PLANES,
        out_shape=[jax.ShapeDtypeStruct((BLOCK, TRIPLE), bf16)] * PLANES,
        compiler_params=params(4),
        name="merge",
    )(info, pltpu.with_memory_space_constraint(over_space, pltpu.HBM), back)


QUARTER = WIDTH // CORES // 2
FAR = PLANES - 1


def hold_kernel(*refs):
    sources, held, sem = refs[: 4 * FAR], refs[4 * FAR], refs[4 * FAR + 1]
    copies = [
        pltpu.make_async_copy(
            source, held.at[n // (2 * FAR) * 2 + n % 2, n % (2 * FAR) // 2], sem.at[n]
        )
        for n, source in enumerate(sources)
    ]
    for copy in copies:
        copy.start()
    for copy in copies:
        copy.wait()


def hold(weights):
    shape = (4, FAR, TRIPLE, QUARTER)
    return pl.pallas_call(
        hold_kernel,
        in_specs=[pl.BlockSpec(memory_space=pltpu.HBM)] * len(weights),
        out_specs=pl.BlockSpec(memory_space=pltpu.VMEM),
        out_shape=pltpu.VMEM(shape, bf16),
        scratch_shapes=[pltpu.SemaphoreType.DMA((4 * FAR,))],
        compiler_params=params(4),
        cost_estimate=pl.CostEstimate(
            flops=1_000_000, bytes_accessed=7_000_000, transcendentals=0
        ),
        name="hold",
    )(*[pltpu.with_memory_space_constraint(w, pltpu.HBM) for w in weights])


def out_kernel(info, r0, r1, r2, r3, own, held, out_ref):
    core = info[3]
    for which in range(CORES):

        @pl.when(core == which)
        def _():
            for q in range(4):
                first = ((which + q // 2) % CORES * 2 + q % 2) * QUARTER
                lanes = slice(first, first + QUARTER)
                total = jnp.dot(r0[...], own[:, lanes], preferred_element_type=f32)
                for k, rows in enumerate((r1, r2, r3)):
                    total += jnp.dot(rows[...], held[q, k], preferred_element_type=f32)
                out_ref[:, lanes] = total.astype(bf16)


def out_project(info, rows, own, held):
    return pl.pallas_call(
        out_kernel,
        in_specs=specs(6),
        out_specs=pl.BlockSpec(memory_space=pltpu.VMEM),
        out_shape=jax.ShapeDtypeStruct((BLOCK, WIDTH), bf16),
        compiler_params=params(8),
        cost_estimate=pl.CostEstimate(
            flops=2 * BLOCK * 1536 * WIDTH, bytes_accessed=10_500_000, transcendentals=0
        ),
        name="out_project",
    )(info, *rows, own, held)


def repeat_kernel(rows_hbm, out_ref, piece, sem):
    copy = pltpu.make_async_copy(
        rows_hbm.at[0, pl.ds(0, TOKEN_PART), pl.ds(HEAD, 2 * HEAD)], piece, sem.at[0]
    )
    copy.start()
    copy.wait()
    out_ref[...] = jnp.broadcast_to(piece[...][None], out_ref.shape)


def repeat_first(rows):
    return pl.pallas_call(
        repeat_kernel,
        in_specs=[pl.BlockSpec(memory_space=pltpu.HBM)],
        out_specs=pl.BlockSpec(memory_space=pltpu.VMEM),
        out_shape=jax.ShapeDtypeStruct((Z, TOKEN_PART, 2 * HEAD), bf16),
        scratch_shapes=[
            pltpu.VMEM((TOKEN_PART, 2 * HEAD), bf16),
            pltpu.SemaphoreType.DMA((1,)),
        ],
        compiler_params=params(4),
        cost_estimate=pl.CostEstimate(flops=0, bytes_accessed=300_000, transcendentals=0),
        name="repeat_first",
    )(rows)


def swap_cores(value):
    return lax.ppermute(value, "core", [(0, 1), (1, 0)])


def shifted(value, axis, count, k):
    return lax.ppermute(value, axis, [(i, (i + k) % count) for i in range(count)])


def local(video_tokens, text_tokens, project_in, project_out, head_class, text_length):
    z, y = lax.axis_index("z"), lax.axis_index("y")
    core, plane = lax.axis_index("core"), lax.axis_index("head")
    here = lax.dynamic_slice_in_dim(head_class, plane * HEADS_HERE, HEADS_HERE)
    info = jnp.concatenate([here, jnp.stack([core, text_length[0], z * Y + y, plane])])

    own_out = project_out.reshape(TRIPLE, WIDTH)
    wide = WIDTH // CORES // 2
    pieces = [
        lax.dynamic_slice_in_dim(own_out, (2 * core + part) * wide, wide, 1) for part in range(2)
    ]

    weights = jnp.transpose(project_in, (1, 0, 2))
    packed = project(video_tokens, text_tokens, weights)
    moved = lax.all_to_all(packed, ("z", "y"), 0, 0, tiled=True)
    partner = swap_cores(packed)

    right = [shifted(p, "head", PLANES, 1) for p in pieces]
    left = [shifted(p, "head", PLANES, PLANES - 1) for p in pieces]
    first_swap = [swap_cores(m) for m in right]
    moved, partner, left, first_swap = lax.optimization_barrier((moved, partner, left, first_swap))
    later_swap = [swap_cores(m) for m in left]
    across = [
        shifted(right[0], "head", PLANES, 1),
        shifted(left[1], "head", PLANES, PLANES - 1),
    ]

    column = lax.all_to_all(repeat_first(moved), "z", 0, 0, tiled=True)
    text_own = moved[:, TOKEN_PART:, :]
    text_other = swap_cores(text_own)
    over_time, text = temporal(info, moved, text_own, text_other)
    column, over_time, later_swap = lax.optimization_barrier((column, over_time, later_swap))
    theirs = first_swap + later_swap
    back = lax.all_to_all(over_time, ("z", "y"), 0, 0, tiled=True)
    columns = [column] + [shifted(column, "y", Y, k) for k in range(1, Y)]
    firsts = columns + [swap_cores(c) for c in columns]

    over_space = spatial(info, packed, partner, firsts, text)
    parts = merge(info, over_space, back)
    mine = right + left + across
    theirs = theirs + [swap_cores(a) for a in across]
    held = hold(mine + theirs)
    gathered = [parts[0]] + [shifted(parts[k], "head", PLANES, k) for k in (1, 3, 2)]
    return out_project(info, gathered, own_out, held)


def solution(mesh):
    split = Mesh(mesh.devices.reshape(Z, Y, CORES, PLANES), ("z", "y", "core", "head"))
    seq = ("z", "y", "core")
    placed = (
        P(seq, None),
        P(seq, None),
        P(None, "head", None),
        P("head", None, None),
        P(),
        P(),
    )
    return jax.shard_map(
        local, mesh=split, in_specs=placed, out_specs=P(seq + ("head",), None), check_vma=False
    )
```

```python
import functools
import math

import jax
import jax.numpy as jnp
from jax import lax
from jax.experimental import pallas as pl
from jax.experimental.pallas import tpu as pltpu
from jax.sharding import Mesh, PartitionSpec as P

Z, Y, CORES, PLANES = 8, 4, 2, 4
CHIPS = Z * Y
HEADS_HERE = 3
HEAD = 128
TRIPLE = 3 * HEAD
ROWS = 512
BLOCK = ROWS // PLANES
PIECE = ROWS // CHIPS
TEXT_HERE = 4
TEXT_CORE = CHIPS * TEXT_HERE
TOKEN_PART = HEADS_HERE * PIECE
CHUNK = TOKEN_PART + 2 * TEXT_HERE
WIDTH = 3072
MASKED = -1e30
FACTOR = HEAD**-0.5 * math.log2(math.e)
MIB = 1024 * 1024

f32 = jnp.float32
bf16 = jnp.bfloat16


def params(mib):
    return pltpu.CompilerParams(vmem_limit_bytes=mib * MIB)


def nt(a, b):
    return lax.dot_general(a, b, (((1,), (1,)), ((), ())), preferred_element_type=f32)


CUTS = ((0, 1536), (1536, 1536))
TALL = ROWS + 16


def project_kernel(x_hbm, text_ref, w_hbm, out_ref, x, w, total, text_rows, x_sem, w_sem):

    def fetch(part):
        depth = pl.ds(*CUTS[part])
        yield pltpu.make_async_copy(x_hbm.at[:, depth], x.at[pl.ds(0, ROWS), depth], x_sem.at[part])
        for h in range(HEADS_HERE):
            lanes = pl.ds(h * TRIPLE, TRIPLE)
            yield pltpu.make_async_copy(
                w_hbm.at[h, depth], w.at[depth, lanes], w_sem.at[part, h]
            )

    for part in range(len(CUTS)):
        for copy in fetch(part):
            copy.start()
    padding = jnp.zeros((TALL - ROWS - TEXT_HERE, WIDTH), f32)
    x[ROWS:, :] = jnp.concatenate([text_ref[...].astype(f32), padding], axis=0).astype(bf16)

    blocks = ((0, 256), (256, TALL))
    for part, (first, depth) in enumerate(CUTS):
        for copy in fetch(part):
            copy.wait()
        for start, stop in blocks:
            partial = jnp.dot(
                x[start:stop, first : first + depth],
                w[first : first + depth, :],
                preferred_element_type=f32,
            )
            if part == 0:
                total[start:stop, :] = partial
                continue
            rows = total[start:stop, :] + partial
            tokens = min(stop, ROWS) - start
            chips = slice(start // PIECE, (start + tokens) // PIECE)
            for h in range(HEADS_HERE):
                piece = rows[:tokens, h * TRIPLE : (h + 1) * TRIPLE].astype(bf16)
                out_ref[chips, h * PIECE : (h + 1) * PIECE, :] = piece.reshape(
                    tokens // PIECE, PIECE, TRIPLE
                )
    for h in range(HEADS_HERE):
        text = rows[tokens : tokens + 8, h * TRIPLE : (h + 1) * TRIPLE]
        lanes = slice(h * HEAD, (h + 1) * HEAD)
        text_rows[0:TEXT_HERE, lanes] = text[0:TEXT_HERE, HEAD : 2 * HEAD]
        text_rows[TEXT_HERE : 2 * TEXT_HERE, lanes] = text[0:TEXT_HERE, 2 * HEAD :]
    out_ref[:, TOKEN_PART:, :] = jnp.broadcast_to(
        text_rows[...].astype(bf16)[None], (CHIPS, 2 * TEXT_HERE, TRIPLE)
    )


def project(video_tokens, text_tokens, weights):
    vmem = pl.BlockSpec(memory_space=pltpu.VMEM)
    hbm = pl.BlockSpec(memory_space=pltpu.HBM)
    return pl.pallas_call(
        project_kernel,
        in_specs=[hbm, vmem, hbm],
        out_specs=vmem,
        out_shape=jax.ShapeDtypeStruct((CHIPS, CHUNK, TRIPLE), bf16),
        scratch_shapes=[
            pltpu.VMEM((TALL, WIDTH), bf16),
            pltpu.VMEM((WIDTH, HEADS_HERE * TRIPLE), bf16),
            pltpu.VMEM((TALL, HEADS_HERE * TRIPLE), f32),
            pltpu.VMEM((2 * TEXT_HERE, TRIPLE), f32),
            pltpu.SemaphoreType.DMA((len(CUTS),)),
            pltpu.SemaphoreType.DMA((len(CUTS), HEADS_HERE)),
        ],
        compiler_params=params(62),
        cost_estimate=pl.CostEstimate(
            flops=2 * ROWS * WIDTH * 3 * TRIPLE, bytes_accessed=12_000_000, transcendentals=0
        ),
        name="project",
    )(video_tokens, text_tokens, weights)


def text_slots(rows, core):
    row = lax.broadcasted_iota(jnp.int32, (rows, TEXT_CORE), 1)
    chip = row & (CHIPS - 1)
    return chip * (CORES * TEXT_HERE) + core * TEXT_HERE + lax.shift_right_logical(row, 5)


def weigh(scores, top, values, total, summed):
    weights = jnp.exp2(scores * FACTOR - top)
    total = total + jnp.sum(weights, axis=1, keepdims=True)
    summed = summed + jnp.dot(weights.astype(bf16), values, preferred_element_type=f32)
    return total, summed


def mask_text(scores, core, length):
    slots = jnp.concatenate(
        [text_slots(scores.shape[0], core), text_slots(scores.shape[0], 1 - core)], axis=1
    )
    return jnp.where(slots < length, scores, MASKED)


def temporal_kernel(info, rows_ref, text_own, text_other, out_ref, text_ref, spread, apart):
    core, length = info[3], info[4]

    for side, source in enumerate((text_own, text_other)):
        for h in range(HEADS_HERE):
            lanes = source[:, :, h * HEAD : (h + 1) * HEAD].astype(f32)
            spread[: CHIPS * 2 * TEXT_HERE, :] = lanes.reshape(CHIPS * 2 * TEXT_HERE, HEAD)
            for kind in range(2):
                for t in range(TEXT_HERE):
                    rows = pl.ds(kind * TEXT_HERE + t, CHIPS, stride=2 * TEXT_HERE)
                    first = side * TEXT_CORE + t * CHIPS
                    text_ref[h, kind, first : first + CHIPS, :] = spread[rows, :].astype(bf16)

    step = apart.shape[0]
    count = step // PIECE
    own = lax.broadcasted_iota(jnp.int32, apart.shape, 0) & (PIECE - 1)
    other = lax.broadcasted_iota(jnp.int32, apart.shape, 1) & (PIECE - 1)
    apart[...] = jnp.where(own == other, 0.0, MASKED)
    for h in range(HEADS_HERE):
        part = slice(h * PIECE, (h + 1) * PIECE)

        @pl.when(info[h] == 0)
        def _():
            keys = rows_ref[:, part, HEAD : 2 * HEAD].reshape(ROWS, HEAD)
            values = rows_ref[:, part, 2 * HEAD :].reshape(ROWS, HEAD)
            for index in range(ROWS // step):
                chips = slice(index * count, (index + 1) * count)
                query = rows_ref[chips, part, :HEAD].reshape(step, HEAD)
                scores = nt(query, keys) + apart[...]
                text = mask_text(nt(query, text_ref[h, 0]), core, length)
                top = FACTOR * jnp.maximum(
                    jnp.max(scores, axis=1, keepdims=True), jnp.max(text, axis=1, keepdims=True)
                )
                total, summed = weigh(scores, top, values, 0.0, 0.0)
                total, summed = weigh(text, top, text_ref[h, 1], total, summed)
                result = (summed / total).astype(bf16)
                out_ref[chips, part, :] = result.reshape(count, PIECE, HEAD)

        @pl.when(info[h] != 0)
        def _():
            out_ref[:, part, :] = jnp.zeros((CHIPS, PIECE, HEAD), bf16)


def specs(count):
    return [pl.BlockSpec(memory_space=pltpu.SMEM)] + [
        pl.BlockSpec(memory_space=pltpu.VMEM)
    ] * count


def temporal(info, rows, text_own, text_other):
    return pl.pallas_call(
        temporal_kernel,
        in_specs=specs(3),
        out_specs=[pl.BlockSpec()] * 2,
        out_shape=[
            pltpu.HBM((CHIPS, TOKEN_PART, HEAD), bf16),
            pltpu.HBM((HEADS_HERE, 2, CORES * TEXT_CORE, HEAD), bf16),
        ],
        scratch_shapes=[
            pltpu.VMEM(((CHIPS + 1) * 2 * TEXT_HERE, HEAD), f32),
            pltpu.VMEM((256, ROWS), f32),
        ],
        compiler_params=params(14),
        cost_estimate=pl.CostEstimate(
            flops=400_000_000, bytes_accessed=3_000_000, transcendentals=1_200_000
        ),
        name="temporal",
    )(info, rows, text_own, text_other)


FRAME_KEYS = 2 * ROWS
VIDEO_KEYS = 2 * FRAME_KEYS
ALL_KEYS = VIDEO_KEYS + CORES * TEXT_CORE


def spatial_kernel(info, own, partner, *refs):
    firsts, (text_ref, out_ref, keys, values) = refs[: 2 * Y], refs[2 * Y :]
    core, length, frame = info[3], info[4], info[5]
    shift = jnp.where(frame == 0, -MASKED, 0.0).astype(f32)
    step = 256
    count = step // PIECE
    for h in range(HEADS_HERE):
        part = slice(h * PIECE, (h + 1) * PIECE)
        head_lanes = slice(h * HEAD, (h + 1) * HEAD)

        @pl.when(info[h] != 0)
        def _():
            place = 0
            for ref in (own, partner, *firsts):
                rows = ref.shape[0] * PIECE
                width = ref.shape[2]
                block = ref[:, part, width - 2 * HEAD :].reshape(rows, 2 * HEAD)
                keys[place : place + rows, :] = block[:, :HEAD]
                values[place : place + rows, :] = block[:, HEAD:]
                place += rows
            keys[VIDEO_KEYS:, :] = text_ref[h, 0]
            values[VIDEO_KEYS:, :] = text_ref[h, 1]

            def body(index, _):
                query = own[pl.ds(index * count, count), part, :HEAD].reshape(step, HEAD)
                here = nt(query, keys[:FRAME_KEYS, :])
                first = nt(query, keys[FRAME_KEYS:VIDEO_KEYS, :])
                text = mask_text(nt(query, keys[VIDEO_KEYS:, :]), core, length)
                top = FACTOR * functools.reduce(
                    jnp.maximum, [jnp.max(s, axis=1, keepdims=True) for s in (here, first, text)]
                )
                total, summed = weigh(here, top, values[:FRAME_KEYS, :], 0.0, 0.0)
                total, summed = weigh(
                    first, top + shift, values[FRAME_KEYS:VIDEO_KEYS, :], total, summed
                )
                total, summed = weigh(text, top, values[VIDEO_KEYS:, :], total, summed)
                rows = pl.ds(pl.multiple_of(index * step, step), step)
                out_ref[rows, head_lanes] = (summed / total).astype(bf16)
                return 0

            lax.fori_loop(0, ROWS // step, body, 0)


def spatial(info, own, partner, firsts, text):
    return pl.pallas_call(
        spatial_kernel,
        in_specs=specs(2 + 2 * Y) + [pl.BlockSpec()],
        out_specs=pl.BlockSpec(),
        out_shape=pltpu.HBM((ROWS, TRIPLE), bf16),
        scratch_shapes=[pltpu.VMEM((ALL_KEYS, HEAD), bf16)] * 2,
        compiler_params=params(20),
        cost_estimate=pl.CostEstimate(
            flops=4_000_000_000, bytes_accessed=1_000_000, transcendentals=0
        ),
        name="spatial",
    )(info, own, partner, *firsts, pltpu.with_memory_space_constraint(text, pltpu.HBM))


def merge_kernel(info, spatial_ref, back, *outs):
    plane = info[6]
    count = CHIPS // PLANES
    for index in range(PLANES):
        step = (index - plane) & (PLANES - 1)
        for k, out_ref in enumerate(outs):

            @pl.when(step == k)
            def _():
                for h in range(HEADS_HERE):
                    lanes = slice(h * HEAD, (h + 1) * HEAD)

                    @pl.when(info[h] != 0)
                    def _():
                        out_ref[:, lanes] = spatial_ref[index * BLOCK : (index + 1) * BLOCK, lanes]

                    @pl.when(info[h] == 0)
                    def _():
                        rows = back[
                            index * count : (index + 1) * count, h * PIECE : (h + 1) * PIECE, :
                        ]
                        out_ref[:, h * HEAD : (h + 1) * HEAD] = rows.reshape(BLOCK, HEAD)


def merge(info, over_space, back):
    return pl.pallas_call(
        merge_kernel,
        in_specs=specs(0) + [pl.BlockSpec()] + specs(1)[1:],
        out_specs=[pl.BlockSpec(memory_space=pltpu.VMEM)] * PLANES,
        out_shape=[jax.ShapeDtypeStruct((BLOCK, TRIPLE), bf16)] * PLANES,
        compiler_params=params(4),
        name="merge",
    )(info, pltpu.with_memory_space_constraint(over_space, pltpu.HBM), back)


QUARTER = WIDTH // CORES // 2
FAR = PLANES - 1


def hold_kernel(*refs):
    sources, held, sem = refs[: 4 * FAR], refs[4 * FAR], refs[4 * FAR + 1]
    copies = [
        pltpu.make_async_copy(
            source, held.at[n // (2 * FAR) * 2 + n % 2, n % (2 * FAR) // 2], sem.at[n]
        )
        for n, source in enumerate(sources)
    ]
    for copy in copies:
        copy.start()
    for copy in copies:
        copy.wait()


def hold(weights):
    shape = (4, FAR, TRIPLE, QUARTER)
    return pl.pallas_call(
        hold_kernel,
        in_specs=[pl.BlockSpec(memory_space=pltpu.HBM)] * len(weights),
        out_specs=pl.BlockSpec(memory_space=pltpu.VMEM),
        out_shape=pltpu.VMEM(shape, bf16),
        scratch_shapes=[pltpu.SemaphoreType.DMA((4 * FAR,))],
        compiler_params=params(4),
        cost_estimate=pl.CostEstimate(
            flops=1_000_000, bytes_accessed=7_000_000, transcendentals=0
        ),
        name="hold",
    )(*[pltpu.with_memory_space_constraint(w, pltpu.HBM) for w in weights])


def out_kernel(info, r0, r1, r2, r3, own, held, out_ref):
    core = info[3]
    for which in range(CORES):

        @pl.when(core == which)
        def _():
            for q in range(4):
                first = ((which + q // 2) % CORES * 2 + q % 2) * QUARTER
                lanes = slice(first, first + QUARTER)
                total = jnp.dot(r0[...], own[:, lanes], preferred_element_type=f32)
                for k, rows in enumerate((r1, r2, r3)):
                    total += jnp.dot(rows[...], held[q, k], preferred_element_type=f32)
                out_ref[:, lanes] = total.astype(bf16)


def out_project(info, rows, own, held):
    return pl.pallas_call(
        out_kernel,
        in_specs=specs(6),
        out_specs=pl.BlockSpec(memory_space=pltpu.VMEM),
        out_shape=jax.ShapeDtypeStruct((BLOCK, WIDTH), bf16),
        compiler_params=params(8),
        cost_estimate=pl.CostEstimate(
            flops=2 * BLOCK * 1536 * WIDTH, bytes_accessed=10_500_000, transcendentals=0
        ),
        name="out_project",
    )(info, *rows, own, held)


def repeat_kernel(rows_hbm, out_ref, piece, sem):
    copy = pltpu.make_async_copy(
        rows_hbm.at[0, pl.ds(0, TOKEN_PART), pl.ds(HEAD, 2 * HEAD)], piece, sem.at[0]
    )
    copy.start()
    copy.wait()
    out_ref[...] = jnp.broadcast_to(piece[...][None], out_ref.shape)


def repeat_first(rows):
    return pl.pallas_call(
        repeat_kernel,
        in_specs=[pl.BlockSpec(memory_space=pltpu.HBM)],
        out_specs=pl.BlockSpec(memory_space=pltpu.VMEM),
        out_shape=jax.ShapeDtypeStruct((Z, TOKEN_PART, 2 * HEAD), bf16),
        scratch_shapes=[
            pltpu.VMEM((TOKEN_PART, 2 * HEAD), bf16),
            pltpu.SemaphoreType.DMA((1,)),
        ],
        compiler_params=params(4),
        cost_estimate=pl.CostEstimate(flops=0, bytes_accessed=300_000, transcendentals=0),
        name="repeat_first",
    )(rows)


def swap_cores(value):
    return lax.ppermute(value, "core", [(0, 1), (1, 0)])


def shifted(value, axis, count, k):
    return lax.ppermute(value, axis, [(i, (i + k) % count) for i in range(count)])


def local(video_tokens, text_tokens, project_in, project_out, head_class, text_length):
    z, y = lax.axis_index("z"), lax.axis_index("y")
    core, plane = lax.axis_index("core"), lax.axis_index("head")
    here = lax.dynamic_slice_in_dim(head_class, plane * HEADS_HERE, HEADS_HERE)
    info = jnp.concatenate([here, jnp.stack([core, text_length[0], z * Y + y, plane])])

    own_out = project_out.reshape(TRIPLE, WIDTH)
    wide = WIDTH // CORES // 2
    pieces = [
        lax.dynamic_slice_in_dim(own_out, (2 * core + part) * wide, wide, 1) for part in range(2)
    ]

    weights = jnp.transpose(project_in, (1, 0, 2))
    packed = project(video_tokens, text_tokens, weights)
    moved = lax.all_to_all(packed, ("z", "y"), 0, 0, tiled=True)
    partner = swap_cores(packed)

    right = [shifted(p, "head", PLANES, 1) for p in pieces]
    left = [shifted(p, "head", PLANES, PLANES - 1) for p in pieces]
    first_swap = [swap_cores(m) for m in right]
    moved, partner, left, first_swap = lax.optimization_barrier((moved, partner, left, first_swap))
    later_swap = [swap_cores(m) for m in left]
    across = [
        shifted(right[0], "head", PLANES, 1),
        shifted(left[1], "head", PLANES, PLANES - 1),
    ]

    column = lax.all_to_all(repeat_first(moved), "z", 0, 0, tiled=True)
    text_own = moved[:, TOKEN_PART:, :]
    text_other = swap_cores(text_own)
    over_time, text = temporal(info, moved, text_own, text_other)
    column, over_time, later_swap = lax.optimization_barrier((column, over_time, later_swap))
    theirs = first_swap + later_swap
    back = lax.all_to_all(over_time, ("z", "y"), 0, 0, tiled=True)
    columns = [column] + [shifted(column, "y", Y, k) for k in range(1, Y)]
    firsts = columns + [swap_cores(c) for c in columns]

    over_space = spatial(info, packed, partner, firsts, text)
    parts = merge(info, over_space, back)
    mine = right + left + across
    theirs = theirs + [swap_cores(a) for a in across]
    held = hold(mine + theirs)
    gathered = [parts[0]] + [shifted(parts[k], "head", PLANES, k) for k in (1, 3, 2)]
    return out_project(info, gathered, own_out, held)


def solution(mesh):
    split = Mesh(mesh.devices.reshape(Z, Y, CORES, PLANES), ("z", "y", "core", "head"))
    seq = ("z", "y", "core")
    placed = (
        P(seq, None),
        P(seq, None),
        P(None, "head", None),
        P("head", None, None),
        P(),
        P(),
    )
    return jax.shard_map(
        local, mesh=split, in_specs=placed, out_specs=P(seq + ("head",), None), check_vma=False
    )
```
